256 devices in a mesh: dp: 16 (over x, y), ctx: 16 (over z, core).
Axes of the slice: x: 4, y: 4, z: 8, core: 2. Of those that a mesh axis runs over, the one named last changes fastest.
Arguments:
- queries: bfloat16 [32768, 4096], P(('dp', 'ctx')), parts along dimension 0, may hold values from -180 to 180
- key_states: bfloat16 [32768, 512], P(('dp', 'ctx')), parts along dimension 0, may hold values from -5 to 5
- value_states: bfloat16 [32768, 512], P(('dp', 'ctx')), parts along dimension 0, may hold values from -6 to 6
- grad_output: bfloat16 [32768, 4096], P(('dp', 'ctx')), parts along dimension 0, may hold values from -6 to 6
- doc_ids: int32 [32768], P('dp'), parts along dimension 0, may hold values from 0 to 3, never falling along the last dimension, each value on 1 to 1024 neighbouring positions
Outputs:
- query_grad: bfloat16 [32768, 4096], P(('dp', 'ctx')), parts along dimension 0
- key_grad: bfloat16 [32768, 512], P(('dp', 'ctx')), parts along dimension 0
- value_grad: bfloat16 [32768, 512], P(('dp', 'ctx')), parts along dimension 0
The draws below stay inside these ranges and needn't reach their ends.
There are 16 independent parts, one for each index of `dp`. The reference program is written for one: setup_inputs(seed, part) draws one part's arguments, and reference() takes and returns one part's arrays. A program takes and returns all parts, laid end to end along the dimension named above; each array names one. Nothing has to cross between parts.
Inputs may be any that keep to these rules, and one draw needn't show every extreme that they name: `doc_ids`: never falls along positions; each document holds 1 to 1024 positions and one holds exactly 1024.
All inputs are finite; a program needn't handle non-finite values.
Results may differ from the reference program's by a relative error of at most 0.029.
Values may be sent and summed in bfloat16 or wider, within the bound.
No kernel may reach another device: no remote copies, remote signals or barrier semaphores. Data moves between devices by JAX's collectives and lax.ppermute only.
A program may use at most 128 MiB of HBM per device.

```python
import math
import jax
import jax.numpy as jnp
import numpy as np
from jax import lax

DH = 128
KVH = 4
GROUP = 8
QH = 32
TOK_DEV = 128
DOCS = 4
TOKENS = 2048
N_CTX = 16


def draw_key_states(key, part):
    key = jax.random.fold_in(key, 11)
    own_draw = jnp.clip(jax.random.normal(key, (TOKENS, KVH * DH), jnp.float32), -5.0, 5.0)
    result = own_draw
    return result.astype(jnp.bfloat16)


def draw_queries(key, part):
    key = jax.random.fold_in(key, 12)
    own_draw = jnp.clip(jax.random.normal(key, (TOKENS, QH * DH), jnp.float32), -5.0, 5.0)
    result = own_draw
    return result.astype(jnp.bfloat16)


def level_of(stream_key, dims, pieces, low, high):
    gain, own = 1.0, jax.random.fold_in(stream_key, 6)
    for dim, blocks in pieces:
        draws = jnp.exp(jax.random.uniform(jax.random.fold_in(own, dim), (blocks,), jnp.float32, low / len(pieces), high / len(pieces)))
        gain = gain * jnp.repeat(draws, dims[dim] // blocks).reshape([-1 if axis == dim else 1 for axis in range(len(dims))])
    return gain


def length_profile(number_of, total, reach, skew):
    loads = [(1 << 20) // math.isqrt(standing ** skew) + 1 for standing in range(2, number_of + 1)]
    spare, holding = total - reach - (number_of - 1), [1] * (number_of - 1)
    while spare > 0:
        free = [i for i in range(number_of - 1) if holding[i] < reach]
        pool, budget = sum([loads[i] for i in free]), spare
        for i in free:
            addition = min(reach - holding[i], max(1, budget * loads[i] // pool), spare)
            holding[i] = holding[i] + addition
            spare = spare - addition
    return np.array([reach] + holding)


def uneven(stream_key, number_of, total, most, slope):
    if number_of == 2:
        one = jax.random.randint(stream_key, (), max(1, total - most), min(most, total - 1) + 1)
        return jnp.stack([one, total - one])
    tallies = jnp.asarray(length_profile(number_of, total, most, slope), jnp.int32)
    pairs = (number_of - 1) // 2
    donor, sink = tallies[1:1 + 2 * pairs:2], tallies[2:2 + 2 * pairs:2]
    room = jnp.minimum(donor - 1, most - sink)
    moved = jax.random.randint(jax.random.fold_in(stream_key, 1), (pairs,), 0, 1 << 20) % (room + 1)
    tallies = tallies.at[1:1 + 2 * pairs:2].set(donor - moved).at[2:2 + 2 * pairs:2].set(sink + moved)
    return tallies[jax.random.permutation(jax.random.fold_in(stream_key, 2), number_of)]


def centred(key, shape, spread, limit, shards=(), held_as=jnp.bfloat16):
    values = jax.random.normal(key, shape, jnp.float32) * spread
    if len(shards) > 0:
        values = level_of(key, shape, shards, -0.22, 0.18) * values
    return jnp.clip(values, min=-limit, max=limit).astype(held_as)


def setup_inputs(seed: int = 0, part: int = 0) -> dict:
    streams_of = jax.random.split(jax.random.key(seed), 6)
    part_keys = jax.random.split(jax.random.fold_in(streams_of[5], part), 6)
    queries = draw_queries(jax.random.fold_in(jax.random.fold_in(streams_of[5], part), 71), part)
    key_states = draw_key_states(jax.random.fold_in(jax.random.fold_in(streams_of[5], part), 71), part)
    value_states = centred(part_keys[2], (TOKENS, KVH * DH), 1.0, 6.0, ((0, 16),))
    grad_output = centred(part_keys[3], (TOKENS, QH * DH), 1.0, 6.0, ((0, 16),))
    doc_ids = jnp.searchsorted(jnp.cumsum(uneven(part_keys[4], DOCS, TOKENS, TOKENS // 2, 0)), jnp.arange(TOKENS), side="right").astype(jnp.int32)
    return {"queries": queries, "key_states": key_states, "value_states": value_states, "grad_output": grad_output, "doc_ids": doc_ids}


NEG = -1.0e30


def storage_order(flat, group_size):
    blocks = flat.reshape(2 * group_size, -1)
    return jnp.stack([blocks[:group_size], blocks[group_size:][::-1]], axis=1).reshape(-1)


def reference(queries, key_states, value_states, grad_output, doc_ids):
    half_rows = TOK_DEV // 2
    scale = DH ** -0.5
    positions = storage_order(jnp.arange(TOKENS, dtype=jnp.int32), N_CTX)
    documents = storage_order(doc_ids.astype(jnp.int32), N_CTX)
    query_blocks = queries.reshape(N_CTX, 2, half_rows, KVH, GROUP, DH)
    grad_blocks = grad_output.reshape(N_CTX, 2, half_rows, KVH, GROUP, DH)
    pos_blocks = positions.reshape(N_CTX, 2, half_rows)
    doc_blocks = documents.reshape(N_CTX, 2, half_rows)
    keys_wide = key_states.reshape(TOKENS, KVH, DH).astype(jnp.float32)
    values_wide = value_states.reshape(TOKENS, KVH, DH).astype(jnp.float32)

    def one_half(query_part, grad_part, pos_part, doc_part):
        query_wide = query_part.astype(jnp.float32)
        grad_wide = grad_part.astype(jnp.float32)
        visible_pairs = (positions[None, :] <= pos_part[:, None]) & (documents[None, :] == doc_part[:, None])
        scores = jnp.einsum("qhgd,khd->hgqk", query_wide, keys_wide) * scale
        scores = jnp.where(visible_pairs[None, None], scores, NEG)
        row_max = jnp.max(scores, axis=-1)
        expo_terms = jnp.where(visible_pairs[None, None], jnp.exp(scores - row_max[..., None]), 0.0)
        log_total = row_max + jnp.log(jnp.sum(expo_terms, axis=-1))
        weights = jnp.where(visible_pairs[None, None], jnp.exp(scores - log_total[..., None]), 0.0)
        grad_prob = jnp.einsum("qhgd,khd->hgqk", grad_wide, values_wide)
        correction = jnp.sum(weights * grad_prob, axis=-1)
        grad_score = (scale * weights * (grad_prob - correction[..., None])).astype(jnp.bfloat16).astype(jnp.float32)
        weights_low = weights.astype(jnp.bfloat16).astype(jnp.float32)
        query_grad = jnp.einsum("hgqk,khd->qhgd", grad_score, keys_wide)
        key_part = jnp.einsum("hgqk,qhgd->khd", grad_score, query_wide)
        value_part = jnp.einsum("hgqk,qhgd->khd", weights_low, grad_wide)
        return query_grad, key_part, value_part

    def one_device(state_now, device_item):
        key_total, value_total = state_now
        query_dev, grad_dev, pos_dev, doc_dev = device_item
        first = one_half(query_dev[0], grad_dev[0], pos_dev[0], doc_dev[0])
        second = one_half(query_dev[1], grad_dev[1], pos_dev[1], doc_dev[1])
        key_part = lax.optimization_barrier((first[1] + second[1]).astype(jnp.bfloat16))
        value_part = lax.optimization_barrier((first[2] + second[2]).astype(jnp.bfloat16))
        key_total = key_total + key_part.astype(jnp.float32)
        value_total = value_total + value_part.astype(jnp.float32)
        return (key_total, value_total), jnp.stack([first[0], second[0]], axis=0)

    zeros_kv = jnp.zeros((TOKENS, KVH, DH), jnp.float32)
    (key_total, value_total), query_grads = lax.scan(one_device, (zeros_kv, zeros_kv), (query_blocks, grad_blocks, pos_blocks, doc_blocks))
    query_grad = query_grads.reshape(TOKENS, KVH * GROUP * DH).astype(jnp.bfloat16)
    key_grad = key_total.reshape(TOKENS, KVH * DH).astype(jnp.bfloat16)
    value_grad = value_total.reshape(TOKENS, KVH * DH).astype(jnp.bfloat16)
    return (query_grad, key_grad, value_grad)
```

```python
import functools

import jax
import jax.numpy as jnp
from jax import lax
from jax.experimental import pallas as pl
from jax.experimental.pallas import tpu as pltpu
from jax.sharding import PartitionSpec as P

DH = 128
GROUP = 8
SCALE = DH ** (-0.5)
LOG2E = 1.4426950408889634
NEG = -1e30
LOW = -1e29
NZ = 8
BLK = 128
NB = 16
LANES = GROUP * BLK
VMEM = 56 * 1024 * 1024

NT = (((1,), (1,)), ((), ()))
NN = (((1,), (0,)), ((), ()))
TN = (((0,), (0,)), ((), ()))


def dot(a, b, dims):
    return lax.dot_general(a, b, dims, preferred_element_type=jnp.float32)


def attention_kernel(
    place, doc_ref, q_ref, do_ref, qd_ref,
    c0, u1, u2, u3, d1, d2, d3, k4, v4,
    dq_own, dq_par, t0, tu1, tu2, tu3, td1, td2, td3, t4,
    qv, dov, kv, qst, dst, acc, dqt, pbuf, gbuf, mbuf, sem,
):
    core, z = place[0], place[1]
    copies = []

    def copy(src, dst):
        copies.append(pltpu.make_async_copy(src, dst, sem.at[len(copies)]))
        copies[-1].start()

    col = pl.multiple_of(core * 2048, 2048)
    copy(q_ref.at[:, pl.ds(col, 2048)], qv.at[0])
    copy(do_ref.at[:, pl.ds(col, 2048)], dov.at[0])
    copy(qd_ref.at[:, pl.ds(0, 2048)], qv.at[1])
    copy(qd_ref.at[:, pl.ds(2048, 2048)], dov.at[1])

    def chip(offset):
        return lax.rem(z + offset + NZ, NZ)

    for chunk, offset in ((c0, 0), (u1, -1), (u2, -2), (u3, -3), (d1, 1), (d2, 2), (d3, 3)):
        s = chip(offset)
        copy(chunk.at[pl.ds(0, BLK)], kv.at[s])
        copy(chunk.at[pl.ds(BLK, BLK)], kv.at[NB - 1 - s])
    far = chip(4)
    for part, low in ((k4, 0), (v4, 256)):
        copy(part.at[pl.ds(0, BLK)], kv.at[far, :, pl.ds(low, 256)])
        copy(part.at[pl.ds(BLK, BLK)], kv.at[NB - 1 - far, :, pl.ds(low, 256)])
    acc[...] = jnp.zeros_like(acc)

    doc = doc_ref[...]
    starts = [jnp.sum((doc < d).astype(jnp.float32)).astype(jnp.int32) for d in (1, 2, 3)]
    for one in copies:
        one.wait()
    for x in range(2):
        for g in range(2):
            for h in range(GROUP):
                cols = slice((g * GROUP + h) * DH, (g * GROUP + h + 1) * DH)
                for half in range(2):
                    rows = slice(h * BLK + half * 64, h * BLK + half * 64 + 64)
                    qst[2 * x + g, rows, :] = qv[half, x * 64:x * 64 + 64, cols]
                    dst[2 * x + g, rows, :] = dov[half, x * 64:x * 64 + 64, cols]

    def one_set(xg, unused):
        x, g = lax.div(xg, 2), lax.rem(xg, 2)
        qb = jnp.where(x == 0, z, NB - 1 - z)
        flip_q = jnp.where(qb < NZ, core, 1 - core)
        lane = lax.broadcasted_iota(jnp.int32, (1, BLK), 1)
        rot = jnp.where(flip_q == 1, lax.rem(lane + 64, BLK), lane)
        doc_row = doc_ref[pl.ds(qb, 1), :]
        doc_row = jnp.where(flip_q == 1, pltpu.roll(doc_row, 64, 1), doc_row)
        pos_q = qb * BLK + rot
        start_q = jnp.where(
            doc_row == 0, 0,
            jnp.where(doc_row == 1, starts[0], jnp.where(doc_row == 2, starts[1], starts[2])),
        )
        low_block = lax.div(jnp.min(start_q), BLK)
        kcol = pl.multiple_of(g * DH, DH)
        vcol = pl.multiple_of(256 + g * DH, DH)

        def first(b, state):
            m, l, d = state
            flip_k = jnp.where(b < NZ, core, 1 - core)
            row = lax.broadcasted_iota(jnp.int32, (BLK, 1), 0)
            pos_k = b * BLK + jnp.where(flip_k == 1, lax.rem(row + 64, BLK), row)
            bias = jnp.where((pos_k <= pos_q) & (pos_k >= start_q), 0.0, NEG)
            bias = jnp.concatenate([bias] * GROUP, axis=1)
            s = dot(kv[b, :, pl.ds(kcol, DH)], qst[xg], NT) * (SCALE * LOG2E) + bias
            new = jnp.maximum(m, jnp.max(s, axis=0, keepdims=True))
            p = jnp.exp2(s - new)
            grad = dot(kv[b, :, pl.ds(vcol, DH)], dst[xg], NT)
            i = b - low_block
            pbuf[i] = p
            gbuf[i] = grad
            mbuf[i] = new
            alpha = jnp.exp2(m - new)
            return (
                new,
                l * alpha + jnp.sum(p, axis=0, keepdims=True),
                d * alpha + jnp.sum(p * grad, axis=0, keepdims=True),
            )

        zero = jnp.zeros((1, LANES), jnp.float32)
        m, l, d = lax.fori_loop(low_block, qb + 1, first, (zero + LOW, zero, zero))
        inv = 1.0 / l
        corr = d * inv
        dqt[...] = jnp.zeros_like(dqt)

        def second(b, unused):
            i = b - low_block
            w = pbuf[i] * (jnp.exp2(mbuf[i] - m) * inv)
            ds = (w * (gbuf[i] - corr)).astype(jnp.bfloat16)
            acc[b, :, pl.ds(kcol, DH)] += dot(ds, qst[xg], NN)
            acc[b, :, pl.ds(vcol, DH)] += dot(w.astype(jnp.bfloat16), dst[xg], NN)
            dqt[...] += dot(kv[b, :, pl.ds(kcol, DH)], ds, TN)
            return 0

        lax.fori_loop(low_block, qb + 1, second, 0)
        rows = pl.multiple_of(x * 64, 64)
        for h in range(GROUP):
            out = jnp.transpose(dqt[:, h * BLK:(h + 1) * BLK] * SCALE).astype(jnp.bfloat16)
            ocol = pl.multiple_of((g * GROUP + h) * DH, DH)
            dq_own[pl.ds(rows, 64), pl.ds(ocol, DH)] = out[:64]
            dq_par[pl.ds(rows, 64), pl.ds(ocol, DH)] = out[64:]
        return 0

    lax.fori_loop(0, 4, one_set, 0)
    for out, offset in (
        (t0, 0), (tu1, 1), (tu2, 2), (tu3, 3), (td1, -1), (td2, -2), (td3, -3), (t4, 4)
    ):
        s = chip(offset)
        for part, b in ((0, s), (1, NB - 1 - s)):
            rows = slice(part * BLK, part * BLK + BLK)
            out[rows, :256] = (acc[b, :, :256] * SCALE).astype(jnp.bfloat16)
            out[rows, 256:] = acc[b, :, 256:].astype(jnp.bfloat16)


def attention(place, doc, queries, grad_output, qd, chunks):
    half = jax.ShapeDtypeStruct((BLK, 2048), jnp.bfloat16)
    term = jax.ShapeDtypeStruct((256, 512), jnp.bfloat16)
    any_space = pl.BlockSpec(memory_space=pl.ANY)
    vmem = pl.BlockSpec(memory_space=pltpu.VMEM)
    return pl.pallas_call(
        attention_kernel,
        out_shape=(half, half) + (term,) * 8,
        in_specs=[pl.BlockSpec(memory_space=pltpu.SMEM), vmem] + [any_space] * 12,
        out_specs=(vmem,) * 10,
        scratch_shapes=[
            pltpu.VMEM((2, BLK, 2048), jnp.bfloat16),
            pltpu.VMEM((2, BLK, 2048), jnp.bfloat16),
            pltpu.VMEM((NB, BLK, 512), jnp.bfloat16),
            pltpu.VMEM((4, LANES, DH), jnp.bfloat16),
            pltpu.VMEM((4, LANES, DH), jnp.bfloat16),
            pltpu.VMEM((NB, BLK, 512), jnp.float32),
            pltpu.VMEM((DH, LANES), jnp.float32),
            pltpu.VMEM((NB // 2 + 1, BLK, LANES), jnp.float32),
            pltpu.VMEM((NB // 2 + 1, BLK, LANES), jnp.float32),
            pltpu.VMEM((NB // 2 + 1, 1, LANES), jnp.float32),
            pltpu.SemaphoreType.DMA((22,)),
        ],
        compiler_params=pltpu.CompilerParams(vmem_limit_bytes=VMEM),
        cost_estimate=pl.CostEstimate(flops=10**10, bytes_accessed=10**7, transcendentals=10**7),
    )(place, doc, queries, grad_output, qd, *chunks)


def ring(step):
    return [(2 * z + c, 2 * ((z + step) % NZ) + c) for z in range(NZ) for c in range(2)]


SWAP = [(i, i ^ 1) for i in range(2 * NZ)]


def send(x, pairs):
    return lax.ppermute(x, "ctx", pairs)


def half_of(x, index):
    width = x.shape[1] // 2
    return lax.dynamic_slice_in_dim(x, index * width, width, 1)


def join(mine, other, core):
    return jnp.where(
        core == 0,
        jnp.concatenate([mine, other], axis=1),
        jnp.concatenate([other, mine], axis=1),
    )


def per_device(queries, key_states, value_states, grad_output, doc_ids):
    index = lax.axis_index("ctx")
    core, z = index % 2, index // 2
    place = jnp.stack([core, z]).astype(jnp.int32)
    doc = doc_ids.reshape(NB, BLK)

    mine = jnp.concatenate([half_of(key_states, core), half_of(value_states, core)], axis=1)
    other = jnp.concatenate([half_of(key_states, 1 - core), half_of(value_states, 1 - core)], axis=1)
    got = send(other, SWAP)
    qd = send(
        jnp.concatenate([half_of(queries, 1 - core), half_of(grad_output, 1 - core)], axis=1), SWAP
    )
    own = jnp.concatenate([mine[:64], got[:64], mine[64:], got[64:]], axis=0)
    up = down = own
    ups, downs = [], []
    for _ in range(3):
        up, down = send(up, ring(1)), send(down, ring(-1))
        ups.append(up)
        downs.append(down)
    far_k, far_v = send(up[:, :256], ring(1)), send(down[:, 256:], ring(-1))

    dq_own, dq_par, t0, tu1, tu2, tu3, td1, td2, td3, t4 = attention(
        place, doc, queries, grad_output, qd, [own, *ups, *downs, far_k, far_v]
    )
    dq_got = send(dq_par, SWAP)

    def add(a, b):
        return (a.astype(jnp.float32) + b.astype(jnp.float32)).astype(jnp.bfloat16)

    up, down = send(t4[:, :256], ring(1)), send(t4[:, 256:], ring(-1))
    up = jnp.concatenate([add(tu3[:, :256], up), tu3[:, 256:]], axis=1)
    down = jnp.concatenate([td3[:, :256], add(td3[:, 256:], down)], axis=1)
    up, down = send(up, ring(1)), send(down, ring(-1))
    up, down = send(add(tu2, up), ring(1)), send(add(td2, down), ring(-1))
    up, down = send(add(tu1, up), ring(1)), send(add(td1, down), ring(-1))
    total = (
        t0.astype(jnp.float32) + up.astype(jnp.float32) + down.astype(jnp.float32)
    ).astype(jnp.bfloat16)
    keep = jnp.concatenate([total[:64], total[128:192]], axis=0)
    away = jnp.concatenate([total[64:128], total[192:]], axis=0)
    back = send(away, SWAP)
    query_grad = join(dq_own, dq_got, core)
    key_grad = join(keep[:, :256], back[:, :256], core)
    value_grad = join(keep[:, 256:], back[:, 256:], core)
    return (query_grad, key_grad, value_grad)


def solution(mesh):
    rows = P(("dp", "ctx"), None)
    return jax.shard_map(
        per_device,
        mesh=mesh,
        in_specs=(rows, rows, rows, rows, P("dp")),
        out_specs=(rows, rows, rows),
        check_vma=False,
    )
```

```python
import functools

import jax
import jax.numpy as jnp
from jax import lax
from jax.experimental import pallas as pl
from jax.experimental.pallas import tpu as pltpu
from jax.sharding import PartitionSpec as P

DH = 128
GROUP = 8
SCALE = DH ** (-0.5)
FACTOR = SCALE * 1.4426950408889634
NEG = -1e30
LOW = -1e29
NZ = 8
BLK = 128
NB = 16
LANES = GROUP * BLK
MIB = 1024 * 1024
BF16 = jnp.bfloat16
F32 = jnp.float32

NT = (((1,), (1,)), ((), ()))
NN = (((1,), (0,)), ((), ()))
TN = (((0,), (0,)), ((), ()))


def dot(a, b, dims):
    return lax.dot_general(a, b, dims, preferred_element_type=F32)


def chip(z, offset):
    return lax.rem(z + offset + NZ, NZ)


def aligned(index, size):
    return pl.multiple_of(index * size, size)


def query_rows(doc_ref, info, qrow):
    core, z = info[0], info[1]
    doc = doc_ref[...]
    starts = [jnp.sum((doc < d).astype(F32)).astype(jnp.int32) for d in (1, 2, 3)]
    lane = lax.broadcasted_iota(jnp.int32, (1, BLK), 1)
    for x in range(2):
        block = z if x == 0 else NB - 1 - z
        flip = core if x == 0 else 1 - core
        rot = jnp.where(flip == 1, lax.rem(lane + 64, BLK), lane)
        doc_row = doc_ref[pl.ds(block, 1), :]
        doc_row = jnp.where(flip == 1, pltpu.roll(doc_row, 64, 1), doc_row)
        start = jnp.where(
            doc_row == 0, 0,
            jnp.where(doc_row == 1, starts[0], jnp.where(doc_row == 2, starts[1], starts[2])),
        )
        qrow[x, 0:1, :] = block * BLK + rot
        qrow[x, 1:2, :] = start
        info[2 + x] = lax.div(jnp.min(start), BLK)


def for_tiles(info, qrow, s, body):
    core, z = info[0], info[1]

    def step(t, unused):
        combo, g = lax.div(t, 2), lax.rem(t, 2)
        x, y = jnp.minimum(combo, 1), lax.div(combo, 2)
        b = jnp.where(y == 0, s, NB - 1 - s)
        qb = jnp.where(x == 0, z, NB - 1 - z)

        @pl.when((b <= qb) & (b >= info[2 + x]))
        def _():
            flip = jnp.where(y == 0, core, 1 - core)
            row = lax.broadcasted_iota(jnp.int32, (BLK, 1), 0)
            pos_k = b * BLK + jnp.where(flip == 1, lax.rem(row + 64, BLK), row)
            seen = (pos_k <= qrow[x, 0:1, :]) & (pos_k >= qrow[x, 1:2, :])
            bias = jnp.where(seen, 0.0, NEG)
            body(x, y, g, jnp.concatenate([bias] * GROUP, axis=1))

        return 0

    lax.fori_loop(0, 6, step, 0)


def stat_tiles(info, qrow, qst, dst, chunk, s, state):
    k_ref, k_col, v_ref, v_col = chunk

    def body(x, y, g, bias):
        i = 2 * x + g
        rows = aligned(y, BLK)
        k = k_ref[pl.ds(rows, BLK), pl.ds(pl.multiple_of(k_col + g * DH, DH), DH)]
        v = v_ref[pl.ds(rows, BLK), pl.ds(pl.multiple_of(v_col + g * DH, DH), DH)]
        score = dot(k, qst[i], NT) * FACTOR + bias
        old = state[i, 0:1, :]
        new = jnp.maximum(old, jnp.max(score, axis=0, keepdims=True))
        p = jnp.exp2(score - new)
        grad = dot(v, dst[i], NT)
        alpha = jnp.exp2(old - new)
        state[i, 0:1, :] = new
        state[i, 1:2, :] = state[i, 1:2, :] * alpha + jnp.sum(p, axis=0, keepdims=True)
        state[i, 2:3, :] = state[i, 2:3, :] * alpha + jnp.sum(p * grad, axis=0, keepdims=True)

    for_tiles(info, qrow, s, body)


def grad_tiles(info, qrow, qst, dst, chunk, s, final, acc, dqt):
    k_ref, k_col, v_ref, v_col = chunk
    acc[...] = jnp.zeros_like(acc)

    def body(x, y, g, bias):
        i = 2 * x + g
        rows = aligned(y, BLK)
        k = k_ref[pl.ds(rows, BLK), pl.ds(pl.multiple_of(k_col + g * DH, DH), DH)]
        v = v_ref[pl.ds(rows, BLK), pl.ds(pl.multiple_of(v_col + g * DH, DH), DH)]
        w = jnp.exp2(dot(k, qst[i], NT) * FACTOR + bias - final[i, 0:1, :])
        ds = (w * (dot(v, dst[i], NT) - final[i, 1:2, :])).astype(BF16)
        acc[pl.ds(rows, BLK), pl.ds(aligned(g, DH), DH)] += dot(ds, qst[i], NN)
        acc[pl.ds(rows, BLK), pl.ds(pl.multiple_of(256 + g * DH, DH), DH)] += dot(
            w.astype(BF16), dst[i], NN
        )
        dqt[i] += dot(k, ds, TN)

    for_tiles(info, qrow, s, body)


def write_terms(acc, key_out, key_col, value_out, value_col):
    key_out[:, key_col:key_col + 256] = (acc[:, :256] * SCALE).astype(BF16)
    value_out[:, value_col:value_col + 256] = acc[:, 256:].astype(BF16)


def whole(ref):
    return (ref, 0, ref, 256)


def open_kernel(place, doc_ref, q_own, do_own, q_par, do_par, own, info, qrow, qst, dst, state):
    info[0] = place[0]
    info[1] = place[1]
    query_rows(doc_ref, info, qrow)
    for x in range(2):
        for g in range(2):
            for h in range(GROUP):
                cols = slice((g * GROUP + h) * DH, (g * GROUP + h + 1) * DH)
                for out, sources in ((qst, (q_own, q_par)), (dst, (do_own, do_par))):
                    for part, source in enumerate(sources):
                        rows = slice(h * BLK + part * 64, h * BLK + part * 64 + 64)
                        out[2 * x + g, rows, :] = source[x * 64:x * 64 + 64, cols]
    for i in range(4):
        state[i, 0:1, :] = jnp.full((1, LANES), LOW, F32)
        state[i, 1:3, :] = jnp.zeros((2, LANES), F32)
    stat_tiles(info, qrow, qst, dst, whole(own), info[1], state)


def stat_kernel(distance, info, qrow, qst, dst, up, down, state_in, state):
    state[...] = state_in[...]
    stat_tiles(info, qrow, qst, dst, whole(up), chip(info[1], -distance), state)
    stat_tiles(info, qrow, qst, dst, whole(down), chip(info[1], distance), state)


def far_kernel(info, qrow, qst, dst, far_k, far_v, state_in, final, tk, tv, dqt, state, acc):
    state[...] = state_in[...]
    s = chip(info[1], 4)
    chunk = (far_k, 0, far_v, 0)
    stat_tiles(info, qrow, qst, dst, chunk, s, state)
    for i in range(4):
        total = state[i, 1:2, :]
        final[i, 0:1, :] = state[i, 0:1, :] + jnp.log2(total)
        final[i, 1:2, :] = state[i, 2:3, :] / total
    dqt[...] = jnp.zeros_like(dqt)
    grad_tiles(info, qrow, qst, dst, chunk, s, final, acc, dqt)
    write_terms(acc, tk, 0, tv, 0)


def grad_kernel(distance, info, qrow, qst, dst, up, down, final, dqt_in, tu, td, dqt, acc):
    dqt[...] = dqt_in[...]
    for chunk, out, offset in ((up, td, -distance), (down, tu, distance)):
        s = chip(info[1], offset)
        grad_tiles(info, qrow, qst, dst, whole(chunk), s, final, acc, dqt)
        write_terms(acc, out, 0, out, 256)


def close_kernel(info, qrow, qst, dst, own, final, dqt_in, t0, dq_own, dq_par, dqt, acc):
    dqt[...] = dqt_in[...]
    grad_tiles(info, qrow, qst, dst, whole(own), info[1], final, acc, dqt)
    write_terms(acc, t0, 0, t0, 256)
    for x in range(2):
        for g in range(2):
            for h in range(GROUP):
                part = dqt[2 * x + g, :, h * BLK:(h + 1) * BLK] * SCALE
                out = jnp.transpose(part).astype(BF16)
                cols = slice((g * GROUP + h) * DH, (g * GROUP + h + 1) * DH)
                dq_own[x * 64:x * 64 + 64, cols] = out[:64]
                dq_par[x * 64:x * 64 + 64, cols] = out[64:]


SMEM_SPEC = pl.BlockSpec(memory_space=pltpu.SMEM)
VMEM_SPEC = pl.BlockSpec(memory_space=pltpu.VMEM)


def shape(dims, dtype=BF16):
    return jax.ShapeDtypeStruct(dims, dtype)


INFO = shape((8,), jnp.int32)
QROW = shape((2, 8, BLK), jnp.int32)
STACK = shape((4, LANES, DH))
STATE = shape((4, 8, LANES), F32)
TERM = shape((256, 512))
HALF_TERM = shape((256, 256))
DQT = shape((4, DH, LANES), F32)
DQ = shape((BLK, 2048))


def call(kernel, out, args, scratch=(), cost=3, limit=24, first_out_smem=False):
    specs = [VMEM_SPEC] * len(out)
    if first_out_smem:
        specs[0] = SMEM_SPEC
    return pl.pallas_call(
        kernel,
        out_shape=tuple(out),
        in_specs=[SMEM_SPEC] + [VMEM_SPEC] * (len(args) - 1),
        out_specs=tuple(specs),
        scratch_shapes=list(scratch),
        compiler_params=pltpu.CompilerParams(vmem_limit_bytes=limit * MIB),
        cost_estimate=pl.CostEstimate(flops=cost * 10**9, bytes_accessed=10**6, transcendentals=0),
    )(*args)


SWAP = [(i, i ^ 1) for i in range(2 * NZ)]


def swap(x):
    return lax.ppermute(x, "ctx", SWAP)


def ring(x, step):
    pairs = [(2 * z + c, 2 * ((z + step) % NZ) + c) for z in range(NZ) for c in range(2)]
    return lax.ppermute(x, "ctx", pairs)


def half_of(x, index):
    width = x.shape[1] // 2
    return lax.dynamic_slice_in_dim(x, index * width, width, 1)


def join(mine, other, core):
    return jnp.where(
        core == 0,
        jnp.concatenate([mine, other], axis=1),
        jnp.concatenate([other, mine], axis=1),
    )


def add(a, b):
    return (a.astype(F32) + b.astype(F32)).astype(BF16)


def per_device(queries, key_states, value_states, grad_output, doc_ids):
    index = lax.axis_index("ctx")
    core, z = index % 2, index // 2
    place = jnp.stack([core, z]).astype(jnp.int32)
    doc = doc_ids.reshape(NB, BLK)

    mine = jnp.concatenate([half_of(key_states, core), half_of(value_states, core)], axis=1)
    other = jnp.concatenate([half_of(key_states, 1 - core), half_of(value_states, 1 - core)], axis=1)
    got = swap(other)
    own = jnp.concatenate([mine[:64], got[:64], mine[64:], got[64:]], axis=0)
    q_in, do_in, unused = lax.optimization_barrier((queries, grad_output, own))
    q_par, do_par = swap(half_of(q_in, 1 - core)), swap(half_of(do_in, 1 - core))
    up = down = own
    ups, downs = [], []
    for _ in range(3):
        up, down = ring(up, 1), ring(down, -1)
        ups.append(up)
        downs.append(down)
    far_k, far_v = ring(up[:, :256], 1), ring(down[:, 256:], -1)

    info, qrow, qst, dst, state = call(
        open_kernel,
        [INFO, QROW, STACK, STACK, STATE],
        [place, doc, half_of(q_in, core), half_of(do_in, core), q_par, do_par, own],
        first_out_smem=True,
    )
    common = [info, qrow, qst, dst]
    for k in (1, 2, 3):
        (state,) = call(
            functools.partial(stat_kernel, k), [STATE], common + [ups[k - 1], downs[k - 1], state]
        )
    acc = pltpu.VMEM((256, 512), F32)
    final, tk, tv, dqt = call(
        far_kernel, [STATE, HALF_TERM, HALF_TERM, DQT], common + [far_k, far_v, state],
        [pltpu.VMEM(STATE.shape, F32), acc],
    )
    up, down = ring(tk, 1), ring(tv, -1)
    for k in (3, 2, 1):
        tu, td, dqt = call(
            functools.partial(grad_kernel, k), [TERM, TERM, DQT],
            common + [ups[k - 1], downs[k - 1], final, dqt], [acc], cost=5,
        )
        if k == 3:
            up = jnp.concatenate([add(tu[:, :256], up), tu[:, 256:]], axis=1)
            down = jnp.concatenate([td[:, :256], add(td[:, 256:], down)], axis=1)
        else:
            up, down = add(tu, up), add(td, down)
        up, down = ring(up, 1), ring(down, -1)
    t0, dq_own, dq_par = call(
        close_kernel, [TERM, DQ, DQ], common + [own, final, dqt],
        [pltpu.VMEM(DQT.shape, F32), acc], cost=5,
    )
    query_grad = join(dq_own, swap(dq_par), core)
    total = (t0.astype(F32) + up.astype(F32) + down.astype(F32)).astype(BF16)
    keep = jnp.concatenate([total[:64], total[128:192]], axis=0)
    away = jnp.concatenate([total[64:128], total[192:]], axis=0)
    back = swap(away)
    key_grad = join(keep[:, :256], back[:, :256], core)
    value_grad = join(keep[:, 256:], back[:, 256:], core)
    return (query_grad, key_grad, value_grad)


def solution(mesh):
    rows = P(("dp", "ctx"), None)
    return jax.shard_map(
        per_device,
        mesh=mesh,
        in_specs=(rows, rows, rows, rows, P("dp")),
        out_specs=(rows, rows, rows),
        check_vma=False,
    )
```

```python
import functools

import jax
import jax.numpy as jnp
from jax import lax
from jax.experimental import pallas as pl
from jax.experimental.pallas import tpu as pltpu
from jax.sharding import PartitionSpec as P

DH = 128
GROUP = 8
SCALE = DH ** (-0.5)
FACTOR = SCALE * 1.4426950408889634
NEG = -1e30
LOW = -1e29
NZ = 8
BLK = 128
NB = 16
LANES = GROUP * BLK
MIB = 1024 * 1024
BF16 = jnp.bfloat16
F32 = jnp.float32

NT = (((1,), (1,)), ((), ()))
NN = (((1,), (0,)), ((), ()))
TN = (((0,), (0,)), ((), ()))


def dot(a, b, dims):
    return lax.dot_general(a, b, dims, preferred_element_type=F32)


def chip(z, offset):
    return lax.rem(z + offset + NZ, NZ)


def aligned(index, size):
    return pl.multiple_of(index * size, size)


def query_rows(doc_ref, info, qrow):
    core, z = info[0], info[1]
    doc = doc_ref[...]
    starts = [jnp.sum((doc < d).astype(F32)).astype(jnp.int32) for d in (1, 2, 3)]
    lane = lax.broadcasted_iota(jnp.int32, (1, BLK), 1)
    for x in range(2):
        block = z if x == 0 else NB - 1 - z
        flip = core if x == 0 else 1 - core
        rot = jnp.where(flip == 1, lax.rem(lane + 64, BLK), lane)
        doc_row = doc_ref[pl.ds(block, 1), :]
        doc_row = jnp.where(flip == 1, pltpu.roll(doc_row, 64, 1), doc_row)
        start = jnp.where(
            doc_row == 0, 0,
            jnp.where(doc_row == 1, starts[0], jnp.where(doc_row == 2, starts[1], starts[2])),
        )
        qrow[x, 0:1, :] = block * BLK + rot
        qrow[x, 1:2, :] = start
        info[2 + x] = lax.div(jnp.min(start), BLK)


def for_tiles(info, qrow, s, body):
    core, z = info[0], info[1]

    def step(t, unused):
        combo, g = lax.div(t, 2), lax.rem(t, 2)
        x, y = jnp.minimum(combo, 1), lax.div(combo, 2)
        b = jnp.where(y == 0, s, NB - 1 - s)
        qb = jnp.where(x == 0, z, NB - 1 - z)

        @pl.when((b <= qb) & (b >= info[2 + x]))
        def _():
            flip = jnp.where(y == 0, core, 1 - core)
            row = lax.broadcasted_iota(jnp.int32, (BLK, 1), 0)
            pos_k = b * BLK + jnp.where(flip == 1, lax.rem(row + 64, BLK), row)
            seen = (pos_k <= qrow[x, 0:1, :]) & (pos_k >= qrow[x, 1:2, :])
            bias = jnp.where(seen, 0.0, NEG)
            body(x, y, g, jnp.concatenate([bias] * GROUP, axis=1))

        return 0

    lax.fori_loop(0, 6, step, 0)


def stat_tiles(info, qrow, qst, dst, chunk, s, state):
    k_ref, k_col, v_ref, v_col = chunk

    def body(x, y, g, bias):
        i = 2 * x + g
        rows = aligned(y, BLK)
        k = k_ref[pl.ds(rows, BLK), pl.ds(pl.multiple_of(k_col + g * DH, DH), DH)]
        v = v_ref[pl.ds(rows, BLK), pl.ds(pl.multiple_of(v_col + g * DH, DH), DH)]
        score = dot(k, qst[i], NT) * FACTOR + bias
        old = state[i, 0:1, :]
        new = jnp.maximum(old, jnp.max(score, axis=0, keepdims=True))
        p = jnp.exp2(score - new)
        grad = dot(v, dst[i], NT)
        alpha = jnp.exp2(old - new)
        state[i, 0:1, :] = new
        state[i, 1:2, :] = state[i, 1:2, :] * alpha + jnp.sum(p, axis=0, keepdims=True)
        state[i, 2:3, :] = state[i, 2:3, :] * alpha + jnp.sum(p * grad, axis=0, keepdims=True)

    for_tiles(info, qrow, s, body)


def grad_tiles(info, qrow, qst, dst, chunk, s, final, acc, dqt):
    k_ref, k_col, v_ref, v_col = chunk
    acc[...] = jnp.zeros_like(acc)

    def body(x, y, g, bias):
        i = 2 * x + g
        rows = aligned(y, BLK)
        k = k_ref[pl.ds(rows, BLK), pl.ds(pl.multiple_of(k_col + g * DH, DH), DH)]
        v = v_ref[pl.ds(rows, BLK), pl.ds(pl.multiple_of(v_col + g * DH, DH), DH)]
        w = jnp.exp2(dot(k, qst[i], NT) * FACTOR + bias - final[i, 0:1, :])
        ds = (w * (dot(v, dst[i], NT) - final[i, 1:2, :])).astype(BF16)
        acc[pl.ds(rows, BLK), pl.ds(aligned(g, DH), DH)] += dot(ds, qst[i], NN)
        acc[pl.ds(rows, BLK), pl.ds(pl.multiple_of(256 + g * DH, DH), DH)] += dot(
            w.astype(BF16), dst[i], NN
        )
        dqt[i] += dot(k, ds, TN)

    for_tiles(info, qrow, s, body)


def write_terms(acc, key_out, key_col, value_out, value_col):
    key_out[:, key_col:key_col + 256] = (acc[:, :256] * SCALE).astype(BF16)
    value_out[:, value_col:value_col + 256] = acc[:, 256:].astype(BF16)


def whole(ref):
    return (ref, 0, ref, 256)


def open_kernel(
    place, doc_ref, q_own, do_own, q_par, do_par, own, info, qrow, qst, dst, state, rows_in, sem
):
    info[0] = place[0]
    info[1] = place[1]
    low = aligned(place[0], 2048)
    copies = [
        pltpu.make_async_copy(source.at[:, pl.ds(low, 2048)], rows_in.at[i], sem.at[i])
        for i, source in enumerate((q_own, do_own, q_par, do_par))
    ]
    for one in copies:
        one.start()
    query_rows(doc_ref, info, qrow)
    for i, one in enumerate(copies):
        one.wait()
        out, part = (qst, dst)[i % 2], i // 2
        for x in range(2):
            for g in range(2):
                for h in range(GROUP):
                    cols = slice((g * GROUP + h) * DH, (g * GROUP + h + 1) * DH)
                    rows = slice(h * BLK + part * 64, h * BLK + part * 64 + 64)
                    out[2 * x + g, rows, :] = rows_in[i, x * 64:x * 64 + 64, cols]
    for i in range(4):
        state[i, 0:1, :] = jnp.full((1, LANES), LOW, F32)
        state[i, 1:3, :] = jnp.zeros((2, LANES), F32)
    stat_tiles(info, qrow, qst, dst, whole(own), info[1], state)


def stat_kernel(distance, info, qrow, qst, dst, up, down, state_in, state):
    state[...] = state_in[...]
    stat_tiles(info, qrow, qst, dst, whole(up), chip(info[1], -distance), state)
    stat_tiles(info, qrow, qst, dst, whole(down), chip(info[1], distance), state)


def far_kernel(info, qrow, qst, dst, far_k, far_v, state_in, final, tk, tv, dqt, state, acc):
    state[...] = state_in[...]
    s = chip(info[1], 4)
    chunk = (far_k, 0, far_v, 0)
    stat_tiles(info, qrow, qst, dst, chunk, s, state)
    for i in range(4):
        total = state[i, 1:2, :]
        final[i, 0:1, :] = state[i, 0:1, :] + jnp.log2(total)
        final[i, 1:2, :] = state[i, 2:3, :] / total
    dqt[...] = jnp.zeros_like(dqt)
    grad_tiles(info, qrow, qst, dst, chunk, s, final, acc, dqt)
    write_terms(acc, tk, 0, tv, 0)


def grad_kernel(distance, info, qrow, qst, dst, up, down, final, dqt_in, tu, td, dqt, acc):
    dqt[...] = dqt_in[...]
    for chunk, out, offset in ((up, td, -distance), (down, tu, distance)):
        s = chip(info[1], offset)
        grad_tiles(info, qrow, qst, dst, whole(chunk), s, final, acc, dqt)
        write_terms(acc, out, 0, out, 256)


def close_kernel(info, qrow, qst, dst, own, final, dqt_in, t0, dq_own, dq_par, dqt, acc):
    dqt[...] = dqt_in[...]
    grad_tiles(info, qrow, qst, dst, whole(own), info[1], final, acc, dqt)
    write_terms(acc, t0, 0, t0, 256)
    for x in range(2):
        for g in range(2):
            for h in range(GROUP):
                part = dqt[2 * x + g, :, h * BLK:(h + 1) * BLK] * SCALE
                out = jnp.transpose(part).astype(BF16)
                cols = slice((g * GROUP + h) * DH, (g * GROUP + h + 1) * DH)
                dq_own[x * 64:x * 64 + 64, cols] = out[:64]
                dq_par[x * 64:x * 64 + 64, cols] = out[64:]


def assemble_kernel(place, mine, got, up, down, own):
    for part, source in ((0, mine), (64, got)):
        for out in (up, down, own):
            out[part:part + 64, :] = source[:64, :]
            out[BLK + part:BLK + part + 64, :] = source[64:, :]


def add_kernel(place, tu, td, up, down, up_out, down_out):
    width = up.shape[1]
    if width < 512:
        up_out[:, width:] = tu[:, width:]
        down_out[:, :512 - width] = td[:, :512 - width]
    cols = slice(0, width)
    up_out[:, cols] = (tu[:, cols].astype(F32) + up[...].astype(F32)).astype(BF16)
    cols = slice(512 - width, 512)
    down_out[:, cols] = (td[:, cols].astype(F32) + down[...].astype(F32)).astype(BF16)


def last_kernel(place, total, back, key, value):
    core = place[0]
    mine, other = aligned(core, 256), aligned(1 - core, 256)
    for out, low in ((key, 0), (value, 256)):
        out[:64, pl.ds(mine, 256)] = total[:64, low:low + 256]
        out[64:, pl.ds(mine, 256)] = total[128:192, low:low + 256]
        out[:, pl.ds(other, 256)] = back[:, low:low + 256]


SMEM_SPEC = pl.BlockSpec(memory_space=pltpu.SMEM)
VMEM_SPEC = pl.BlockSpec(memory_space=pltpu.VMEM)
ANY_SPEC = pl.BlockSpec(memory_space=pltpu.HBM)


def shape(dims, dtype=BF16):
    return jax.ShapeDtypeStruct(dims, dtype)


INFO = shape((8,), jnp.int32)
QROW = shape((2, 8, BLK), jnp.int32)
STACK = shape((4, LANES, DH))
STATE = shape((4, 8, LANES), F32)
TERM = shape((256, 512))
HALF_TERM = shape((256, 256))
DQT = shape((4, DH, LANES), F32)
DQ = shape((BLK, 2048))


def call(kernel, out, args, scratch=(), cost=3, limit=24, first_out_smem=False, far=()):
    in_specs = [SMEM_SPEC] + [
        ANY_SPEC if i in far else VMEM_SPEC for i in range(1, len(args))
    ]
    specs = [VMEM_SPEC] * len(out)
    if first_out_smem:
        specs[0] = SMEM_SPEC
    return pl.pallas_call(
        kernel,
        out_shape=tuple(out),
        in_specs=in_specs,
        out_specs=tuple(specs),
        scratch_shapes=list(scratch),
        compiler_params=pltpu.CompilerParams(vmem_limit_bytes=limit * MIB),
        cost_estimate=pl.CostEstimate(flops=cost * 10**9, bytes_accessed=10**6, transcendentals=0),
    )(*args)


SWAP = [(i, i ^ 1) for i in range(2 * NZ)]


def swap(x):
    return lax.ppermute(x, "ctx", SWAP)


def ring(x, step):
    pairs = [(2 * z + c, 2 * ((z + step) % NZ) + c) for z in range(NZ) for c in range(2)]
    return lax.ppermute(x, "ctx", pairs)


def half_of(x, index):
    width = x.shape[1] // 2
    return lax.dynamic_slice_in_dim(x, index * width, width, 1)


def join(mine, other, core):
    return jnp.where(
        core == 0,
        jnp.concatenate([mine, other], axis=1),
        jnp.concatenate([other, mine], axis=1),
    )


def add(a, b):
    return (a.astype(F32) + b.astype(F32)).astype(BF16)


def per_device(queries, key_states, value_states, grad_output, doc_ids):
    index = lax.axis_index("ctx")
    core, z = index % 2, index // 2
    place = jnp.stack([core, z]).astype(jnp.int32)
    doc = doc_ids.reshape(NB, BLK)

    mine = jnp.concatenate([half_of(key_states, core), half_of(value_states, core)], axis=1)
    other = jnp.concatenate([half_of(key_states, 1 - core), half_of(value_states, 1 - core)], axis=1)
    got = swap(other)
    own_up, own_down, own = call(assemble_kernel, [TERM] * 3, [place, mine, got])
    together = lax.optimization_barrier
    q_in, do_in, unused = together((queries, grad_output, got))
    q_par, do_par = swap(q_in), swap(do_in)
    up, down = ring(own_up, 1), ring(own_down, -1)
    info, qrow, qst, dst, state = call(
        open_kernel,
        [INFO, QROW, STACK, STACK, STATE],
        [place, doc, queries, grad_output, q_par, do_par, own],
        [pltpu.VMEM((4, BLK, 2048), BF16), pltpu.SemaphoreType.DMA((4,))],
        first_out_smem=True, far=(2, 3, 4, 5),
    )
    common = [info, qrow, qst, dst]
    ups, downs = [], []
    for k in (1, 2, 3):
        up, down, state = together((up, down, state))
        ups.append(up)
        downs.append(down)
        if k < 3:
            next_up, next_down = ring(up, 1), ring(down, -1)
        else:
            far_up, far_down = together((up[:, :256], down[:, 256:]))
            next_up, next_down = ring(far_up, 1), ring(far_down, -1)
        (state,) = call(
            functools.partial(stat_kernel, k), [STATE], common + [up, down, state]
        )
        up, down = next_up, next_down
    far_k, far_v = up, down
    acc = pltpu.VMEM((256, 512), F32)
    final, tk, tv, dqt = call(
        far_kernel, [STATE, HALF_TERM, HALF_TERM, DQT], common + [far_k, far_v, state],
        [pltpu.VMEM(STATE.shape, F32), acc],
    )
    up, down = ring(tk, 1), ring(tv, -1)
    for k in (3, 2, 1):
        tu, td, dqt = call(
            functools.partial(grad_kernel, k), [TERM, TERM, DQT],
            common + [ups[k - 1], downs[k - 1], final, dqt], [acc], cost=5,
        )
        up, down, tu, td, dqt = together((up, down, tu, td, dqt))
        if k == 3:
            up = jnp.concatenate([add(tu[:, :256], up), tu[:, 256:]], axis=1)
            down = jnp.concatenate([td[:, :256], add(td[:, 256:], down)], axis=1)
        else:
            up, down = add(tu, up), add(td, down)
        up, down = together((up, down))
        up, down = ring(up, 1), ring(down, -1)
    t0, dq_own, dq_par = call(
        close_kernel, [TERM, DQ, DQ], common + [own, final, dqt],
        [pltpu.VMEM(DQT.shape, F32), acc], cost=5,
    )
    dq_got = swap(dq_par)
    total = (t0.astype(F32) + up.astype(F32) + down.astype(F32)).astype(BF16)
    away = jnp.concatenate([total[64:128], total[192:]], axis=0)
    away, dq_own = together((away, dq_own))
    back = swap(away)
    query_grad, total = together((join(dq_own, dq_got, core), total))
    key_grad, value_grad = call(last_kernel, [shape((BLK, 512))] * 2, [place, total, back])
    return (query_grad, key_grad, value_grad)


def solution(mesh):
    rows = P(("dp", "ctx"), None)
    return jax.shard_map(
        per_device,
        mesh=mesh,
        in_specs=(rows, rows, rows, rows, P("dp")),
        out_specs=(rows, rows, rows),
        check_vma=False,
    )
```

```python
import functools

import jax
import jax.numpy as jnp
from jax import lax
from jax.experimental import pallas as pl
from jax.experimental.pallas import tpu as pltpu
from jax.sharding import PartitionSpec as P

DH = 128
GROUP = 8
SCALE = DH ** (-0.5)
FACTOR = SCALE * 1.4426950408889634
NEG = -1e30
LOW = -1e29
NZ = 8
BLK = 128
NB = 16
LANES = GROUP * BLK
MIB = 1024 * 1024
BF16 = jnp.bfloat16
F32 = jnp.float32

NT = (((1,), (1,)), ((), ()))
NN = (((1,), (0,)), ((), ()))
TN = (((0,), (0,)), ((), ()))


def dot(a, b, dims):
    return lax.dot_general(a, b, dims, preferred_element_type=F32)


def chip(z, offset):
    return lax.rem(z + offset + NZ, NZ)


def aligned(index, size):
    return pl.multiple_of(index * size, size)


def query_rows(doc_ref, info, qrow):
    core, z = info[0], info[1]
    doc = doc_ref[...]
    starts = [jnp.sum((doc < d).astype(F32)).astype(jnp.int32) for d in (1, 2, 3)]
    lane = lax.broadcasted_iota(jnp.int32, (1, BLK), 1)
    for x in range(2):
        block = z if x == 0 else NB - 1 - z
        flip = core if x == 0 else 1 - core
        rot = jnp.where(flip == 1, lax.rem(lane + 64, BLK), lane)
        doc_row = doc_ref[pl.ds(block, 1), :]
        doc_row = jnp.where(flip == 1, pltpu.roll(doc_row, 64, 1), doc_row)
        start = jnp.where(
            doc_row == 0, 0,
            jnp.where(doc_row == 1, starts[0], jnp.where(doc_row == 2, starts[1], starts[2])),
        )
        qrow[x, 0:1, :] = block * BLK + rot
        qrow[x, 1:2, :] = start
        info[2 + x] = lax.div(jnp.min(start), BLK)


def for_tiles(info, qrow, s, body):
    core, z = info[0], info[1]

    def step(t, unused):
        combo, g = lax.div(t, 2), lax.rem(t, 2)
        x, y = jnp.minimum(combo, 1), lax.div(combo, 2)
        b = jnp.where(y == 0, s, NB - 1 - s)
        qb = jnp.where(x == 0, z, NB - 1 - z)

        @pl.when((b <= qb) & (b >= info[2 + x]))
        def _():
            flip = jnp.where(y == 0, core, 1 - core)
            row = lax.broadcasted_iota(jnp.int32, (BLK, 1), 0)
            pos_k = b * BLK + jnp.where(flip == 1, lax.rem(row + 64, BLK), row)
            seen = (pos_k <= qrow[x, 0:1, :]) & (pos_k >= qrow[x, 1:2, :])
            bias = jnp.where(seen, 0.0, NEG)
            body(t, x, y, g, jnp.concatenate([bias] * GROUP, axis=1))

        return 0

    lax.fori_loop(0, 6, step, 0)


def stat_tiles(info, qrow, qst, dst, chunk, s, state):
    k_ref, k_col, v_ref, v_col = chunk

    def body(t, x, y, g, bias):
        i = 2 * x + g
        rows = aligned(y, BLK)
        k = k_ref[pl.ds(rows, BLK), pl.ds(pl.multiple_of(k_col + g * DH, DH), DH)]
        v = v_ref[pl.ds(rows, BLK), pl.ds(pl.multiple_of(v_col + g * DH, DH), DH)]
        score = dot(k, qst[i], NT) * FACTOR + bias
        old = state[i, 0:1, :]
        new = jnp.maximum(old, jnp.max(score, axis=0, keepdims=True))
        p = jnp.exp2(score - new)
        grad = dot(v, dst[i], NT)
        alpha = jnp.exp2(old - new)
        state[i, 0:1, :] = new
        state[i, 1:2, :] = state[i, 1:2, :] * alpha + jnp.sum(p, axis=0, keepdims=True)
        state[i, 2:3, :] = state[i, 2:3, :] * alpha + jnp.sum(p * grad, axis=0, keepdims=True)

    for_tiles(info, qrow, s, body)


def grad_tiles(info, qrow, qst, dst, chunk, s, final, acc, dqt):
    k_ref, k_col, v_ref, v_col = chunk
    acc[...] = jnp.zeros_like(acc)

    def body(t, x, y, g, bias):
        i = 2 * x + g
        rows = aligned(y, BLK)
        k = k_ref[pl.ds(rows, BLK), pl.ds(pl.multiple_of(k_col + g * DH, DH), DH)]
        v = v_ref[pl.ds(rows, BLK), pl.ds(pl.multiple_of(v_col + g * DH, DH), DH)]
        w = jnp.exp2(dot(k, qst[i], NT) * FACTOR + bias - final[i, 0:1, :])
        ds = (w * (dot(v, dst[i], NT) - final[i, 1:2, :])).astype(BF16)
        acc[pl.ds(rows, BLK), pl.ds(aligned(g, DH), DH)] += dot(ds, qst[i], NN)
        acc[pl.ds(rows, BLK), pl.ds(pl.multiple_of(256 + g * DH, DH), DH)] += dot(
            w.astype(BF16), dst[i], NN
        )
        dqt[i] += dot(k, ds, TN)

    for_tiles(info, qrow, s, body)


def write_terms(acc, key_out, key_col, value_out, value_col):
    key_out[:, key_col:key_col + 256] = (acc[:, :256] * SCALE).astype(BF16)
    value_out[:, value_col:value_col + 256] = acc[:, 256:].astype(BF16)


def whole(ref):
    return (ref, 0, ref, 256)


def open_kernel(
    place, doc_ref, q_own, do_own, q_par, do_par, own, info, qrow, qst, dst, state, rows_in, sem
):
    info[0] = place[0]
    info[1] = place[1]
    low = aligned(place[0], 2048)
    copies = [
        pltpu.make_async_copy(source.at[:, pl.ds(low, 2048)], rows_in.at[i], sem.at[i])
        for i, source in enumerate((q_own, do_own, q_par, do_par))
    ]
    for one in copies:
        one.start()
    query_rows(doc_ref, info, qrow)
    for i, one in enumerate(copies):
        one.wait()
        out, part = (qst, dst)[i % 2], i // 2
        for x in range(2):
            for g in range(2):
                for h in range(GROUP):
                    cols = slice((g * GROUP + h) * DH, (g * GROUP + h + 1) * DH)
                    rows = slice(h * BLK + part * 64, h * BLK + part * 64 + 64)
                    out[2 * x + g, rows, :] = rows_in[i, x * 64:x * 64 + 64, cols]
    for i in range(4):
        state[i, 0:1, :] = jnp.full((1, LANES), LOW, F32)
        state[i, 1:3, :] = jnp.zeros((2, LANES), F32)
    stat_tiles(info, qrow, qst, dst, whole(own), info[1], state)


def stat_kernel(distance, info, qrow, qst, dst, up, down, state_in, state):
    state[...] = state_in[...]
    stat_tiles(info, qrow, qst, dst, whole(up), chip(info[1], -distance), state)
    stat_tiles(info, qrow, qst, dst, whole(down), chip(info[1], distance), state)


def far_kernel(
    info, qrow, qst, dst, far_k, far_v, state_in, final, tk, tv, ds_out,
    state, acc, probs, grads, maxes,
):
    state[...] = state_in[...]
    acc[...] = jnp.zeros_like(acc)
    s = chip(info[1], 4)

    def first(t, x, y, g, bias):
        i = 2 * x + g
        rows, cols = aligned(y, BLK), aligned(g, DH)
        score = dot(far_k[pl.ds(rows, BLK), pl.ds(cols, DH)], qst[i], NT) * FACTOR + bias
        old = state[i, 0:1, :]
        new = jnp.maximum(old, jnp.max(score, axis=0, keepdims=True))
        p = jnp.exp2(score - new)
        grad = dot(far_v[pl.ds(rows, BLK), pl.ds(cols, DH)], dst[i], NT)
        alpha = jnp.exp2(old - new)
        probs[t] = p
        grads[t] = grad
        maxes[t, 0:1, :] = new
        state[i, 0:1, :] = new
        state[i, 1:2, :] = state[i, 1:2, :] * alpha + jnp.sum(p, axis=0, keepdims=True)
        state[i, 2:3, :] = state[i, 2:3, :] * alpha + jnp.sum(p * grad, axis=0, keepdims=True)

    for_tiles(info, qrow, s, first)
    for i in range(4):
        total = state[i, 1:2, :]
        final[i, 0:1, :] = state[i, 0:1, :] + jnp.log2(total)
        final[i, 1:2, :] = state[i, 2:3, :] / total

    def second(t, x, y, g, bias):
        i = 2 * x + g
        rows, cols = aligned(y, BLK), aligned(g, DH)
        w = probs[t] * jnp.exp2(maxes[t, 0:1, :] - final[i, 0:1, :])
        ds = (w * (grads[t] - final[i, 1:2, :])).astype(BF16)
        ds_out[t] = ds
        acc[pl.ds(rows, BLK), pl.ds(cols, DH)] += dot(ds, qst[i], NN)
        acc[pl.ds(rows, BLK), pl.ds(pl.multiple_of(256 + g * DH, DH), DH)] += dot(
            w.astype(BF16), dst[i], NN
        )

    for_tiles(info, qrow, s, second)
    write_terms(acc, tk, 0, tv, 0)


def far_query_kernel(info, qrow, far_k, ds_in, dqt):
    dqt[...] = jnp.zeros_like(dqt)

    def body(t, x, y, g, bias):
        k = far_k[pl.ds(aligned(y, BLK), BLK), pl.ds(aligned(g, DH), DH)]
        dqt[2 * x + g] += dot(k, ds_in[t], TN)

    for_tiles(info, qrow, chip(info[1], 4), body)


def third_kernel(info, qrow, qst, dst, up, down, final, far_k, ds_in, tu, td, dqt, acc):
    far_query_kernel(info, qrow, far_k, ds_in, dqt)
    grad_pair(3, info, qrow, qst, dst, up, down, final, tu, td, dqt, acc)


def grad_kernel(distance, info, qrow, qst, dst, up, down, final, dqt_in, tu, td, dqt, acc):
    dqt[...] = dqt_in[...]
    grad_pair(distance, info, qrow, qst, dst, up, down, final, tu, td, dqt, acc)


def grad_pair(distance, info, qrow, qst, dst, up, down, final, tu, td, dqt, acc):
    for chunk, out, offset in ((up, td, -distance), (down, tu, distance)):
        s = chip(info[1], offset)
        grad_tiles(info, qrow, qst, dst, whole(chunk), s, final, acc, dqt)
        write_terms(acc, out, 0, out, 256)


def close_kernel(info, qrow, qst, dst, own, final, dqt_in, t0, dq_own, dq_par, dqt, acc):
    dqt[...] = dqt_in[...]
    grad_tiles(info, qrow, qst, dst, whole(own), info[1], final, acc, dqt)
    write_terms(acc, t0, 0, t0, 256)
    for x in range(2):
        for g in range(2):
            for h in range(GROUP):
                part = dqt[2 * x + g, :, h * BLK:(h + 1) * BLK] * SCALE
                out = jnp.transpose(part).astype(BF16)
                cols = slice((g * GROUP + h) * DH, (g * GROUP + h + 1) * DH)
                dq_own[x * 64:x * 64 + 64, cols] = out[:64]
                dq_par[x * 64:x * 64 + 64, cols] = out[64:]


def assemble_kernel(place, mine, got, up, down, own):
    for part, source in ((0, mine), (64, got)):
        for out in (up, down, own):
            out[part:part + 64, :] = source[:64, :]
            out[BLK + part:BLK + part + 64, :] = source[64:, :]


def add_kernel(place, tu, td, up, down, up_out, down_out):
    width = up.shape[1]
    if width < 512:
        up_out[:, width:] = tu[:, width:]
        down_out[:, :512 - width] = td[:, :512 - width]
    cols = slice(0, width)
    up_out[:, cols] = (tu[:, cols].astype(F32) + up[...].astype(F32)).astype(BF16)
    cols = slice(512 - width, 512)
    down_out[:, cols] = (td[:, cols].astype(F32) + down[...].astype(F32)).astype(BF16)


def last_kernel(place, total, back, key, value, sem):
    core = place[0]
    mine, other = aligned(core, 256), aligned(1 - core, 256)
    copies = []
    for out, low in ((key, 0), (value, 256)):
        cols = pl.ds(low, 256)
        for source, target in (
            (total.at[pl.ds(0, 64), cols], out.at[pl.ds(0, 64), pl.ds(mine, 256)]),
            (total.at[pl.ds(128, 64), cols], out.at[pl.ds(64, 64), pl.ds(mine, 256)]),
            (back.at[:, cols], out.at[:, pl.ds(other, 256)]),
        ):
            copies.append(pltpu.make_async_copy(source, target, sem.at[len(copies)]))
            copies[-1].start()
    for one in copies:
        one.wait()


SMEM_SPEC = pl.BlockSpec(memory_space=pltpu.SMEM)
VMEM_SPEC = pl.BlockSpec(memory_space=pltpu.VMEM)
ANY_SPEC = pl.BlockSpec(memory_space=pltpu.HBM)


def shape(dims, dtype=BF16):
    return jax.ShapeDtypeStruct(dims, dtype)


INFO = shape((8,), jnp.int32)
QROW = shape((2, 8, BLK), jnp.int32)
STACK = shape((4, LANES, DH))
STATE = shape((4, 8, LANES), F32)
TERM = shape((256, 512))
HALF_TERM = shape((256, 256))
DQT = shape((4, DH, LANES), F32)
DQ = shape((BLK, 2048))


def call(kernel, out, args, scratch=(), cost=3, limit=24, first_out_smem=False, far=(), far_out=False):
    in_specs = [SMEM_SPEC] + [
        ANY_SPEC if i in far else VMEM_SPEC for i in range(1, len(args))
    ]
    specs = [ANY_SPEC if far_out else VMEM_SPEC] * len(out)
    if first_out_smem:
        specs[0] = SMEM_SPEC
    return pl.pallas_call(
        kernel,
        out_shape=tuple(out),
        in_specs=in_specs,
        out_specs=tuple(specs),
        scratch_shapes=list(scratch),
        compiler_params=pltpu.CompilerParams(vmem_limit_bytes=limit * MIB),
        cost_estimate=pl.CostEstimate(flops=cost * 10**9, bytes_accessed=10**6, transcendentals=0),
    )(*args)


SWAP = [(i, i ^ 1) for i in range(2 * NZ)]


def swap(x):
    return lax.ppermute(x, "ctx", SWAP)


def ring(x, step):
    pairs = [(2 * z + c, 2 * ((z + step) % NZ) + c) for z in range(NZ) for c in range(2)]
    return lax.ppermute(x, "ctx", pairs)


def half_of(x, index):
    width = x.shape[1] // 2
    return lax.dynamic_slice_in_dim(x, index * width, width, 1)


def join(mine, other, core):
    return jnp.where(
        core == 0,
        jnp.concatenate([mine, other], axis=1),
        jnp.concatenate([other, mine], axis=1),
    )


def add(a, b):
    return (a.astype(F32) + b.astype(F32)).astype(BF16)


def per_device(queries, key_states, value_states, grad_output, doc_ids):
    index = lax.axis_index("ctx")
    core, z = index % 2, index // 2
    place = jnp.stack([core, z]).astype(jnp.int32)
    doc = doc_ids.reshape(NB, BLK)

    mine = jnp.concatenate([half_of(key_states, core), half_of(value_states, core)], axis=1)
    other = jnp.concatenate([half_of(key_states, 1 - core), half_of(value_states, 1 - core)], axis=1)
    got = swap(other)
    own_up, own_down, own = call(assemble_kernel, [TERM] * 3, [place, mine, got])
    together = lax.optimization_barrier
    q_in, do_in, unused = together((queries, grad_output, got))
    q_par, do_par = swap(q_in), swap(do_in)
    up, down = ring(own_up, 1), ring(own_down, -1)
    info, qrow, qst, dst, state = call(
        open_kernel,
        [INFO, QROW, STACK, STACK, STATE],
        [place, doc, queries, grad_output, q_par, do_par, own],
        [pltpu.VMEM((4, BLK, 2048), BF16), pltpu.SemaphoreType.DMA((4,))],
        first_out_smem=True, far=(2, 3, 4, 5),
    )
    common = [info, qrow, qst, dst]
    ups, downs = [], []
    for k in (1, 2, 3):
        up, down, state = together((up, down, state))
        ups.append(up)
        downs.append(down)
        if k < 3:
            next_up, next_down = ring(up, 1), ring(down, -1)
        else:
            far_up, far_down = together((up[:, :256], down[:, 256:]))
            next_up, next_down = ring(far_up, 1), ring(far_down, -1)
        (state,) = call(
            functools.partial(stat_kernel, k), [STATE], common + [up, down, state]
        )
        up, down = next_up, next_down
    far_k, far_v = up, down
    acc = pltpu.VMEM((256, 512), F32)
    tiles = (6, BLK, LANES)
    final, tk, tv, ds_far = call(
        far_kernel, [STATE, HALF_TERM, HALF_TERM, shape(tiles)], common + [far_k, far_v, state],
        [pltpu.VMEM(STATE.shape, F32), acc, pltpu.VMEM(tiles, F32), pltpu.VMEM(tiles, F32),
         pltpu.VMEM((6, 8, LANES), F32)],
    )
    up, down = ring(tk, 1), ring(tv, -1)
    for k in (3, 2, 1):
        chunks = common + [ups[k - 1], downs[k - 1], final]
        outs = [TERM, TERM, DQT]
        if k == 3:
            tu, td, dqt = call(third_kernel, outs, chunks + [far_k, ds_far], [acc], cost=5)
        else:
            tu, td, dqt = call(
                functools.partial(grad_kernel, k), outs, chunks + [dqt], [acc], cost=5
            )
        up, down, tu, td, dqt = together((up, down, tu, td, dqt))
        if k == 3:
            up = jnp.concatenate([add(tu[:, :256], up), tu[:, 256:]], axis=1)
            down = jnp.concatenate([td[:, :256], add(td[:, 256:], down)], axis=1)
        else:
            up, down = add(tu, up), add(td, down)
        up, down = together((up, down))
        up, down = ring(up, 1), ring(down, -1)
    t0, dq_own, dq_par = call(
        close_kernel, [TERM, DQ, DQ], common + [own, final, dqt],
        [pltpu.VMEM(DQT.shape, F32), acc], cost=5,
    )
    dq_got = swap(dq_par)
    total = (t0.astype(F32) + up.astype(F32) + down.astype(F32)).astype(BF16)
    away = jnp.concatenate([total[64:128], total[192:]], axis=0)
    away, dq_own = together((away, dq_own))
    back = swap(away)
    query_grad, total = together((join(dq_own, dq_got, core), total))
    key_grad, value_grad = call(
        last_kernel, [shape((BLK, 512))] * 2, [place, total, back],
        [pltpu.SemaphoreType.DMA((6,))], far_out=True,
    )
    return (query_grad, key_grad, value_grad)


def solution(mesh):
    rows = P(("dp", "ctx"), None)
    return jax.shard_map(
        per_device,
        mesh=mesh,
        in_specs=(rows, rows, rows, rows, P("dp")),
        out_specs=(rows, rows, rows),
        check_vma=False,
    )
```

```python
import functools

import jax
import jax.numpy as jnp
from jax import lax
from jax.experimental import pallas as pl
from jax.experimental.pallas import tpu as pltpu
from jax.sharding import PartitionSpec as P

DH = 128
GROUP = 8
SCALE = DH ** (-0.5)
FACTOR = SCALE * 1.4426950408889634
NEG = -1e30
LOW = -1e29
NZ = 8
BLK = 128
NB = 16
LANES = GROUP * BLK
MIB = 1024 * 1024
BF16 = jnp.bfloat16
F32 = jnp.float32

NT = (((1,), (1,)), ((), ()))
NN = (((1,), (0,)), ((), ()))
TN = (((0,), (0,)), ((), ()))


def dot(a, b, dims):
    return lax.dot_general(a, b, dims, preferred_element_type=F32)


def chip(z, offset):
    return lax.rem(z + offset + NZ, NZ)


def aligned(index, size):
    return pl.multiple_of(index * size, size)


def query_rows(doc_ref, info, qrow):
    core, z = info[0], info[1]
    doc = doc_ref[...]
    starts = [jnp.sum((doc < d).astype(F32)).astype(jnp.int32) for d in (1, 2, 3)]
    lane = lax.broadcasted_iota(jnp.int32, (1, BLK), 1)
    for x in range(2):
        block = z if x == 0 else NB - 1 - z
        flip = core if x == 0 else 1 - core
        rot = jnp.where(flip == 1, lax.rem(lane + 64, BLK), lane)
        doc_row = doc_ref[pl.ds(block, 1), :]
        doc_row = jnp.where(flip == 1, pltpu.roll(doc_row, 64, 1), doc_row)
        start = jnp.where(
            doc_row == 0, 0,
            jnp.where(doc_row == 1, starts[0], jnp.where(doc_row == 2, starts[1], starts[2])),
        )
        qrow[x, 0:1, :] = block * BLK + rot
        qrow[x, 1:2, :] = start
        info[2 + x] = lax.div(jnp.min(start), BLK)


def for_tiles(info, qrow, s, body):
    core, z = info[0], info[1]

    def step(t, unused):
        combo, g = lax.div(t, 2), lax.rem(t, 2)
        x, y = jnp.minimum(combo, 1), lax.div(combo, 2)
        b = jnp.where(y == 0, s, NB - 1 - s)
        qb = jnp.where(x == 0, z, NB - 1 - z)

        @pl.when((b <= qb) & (b >= info[2 + x]))
        def _():
            flip = jnp.where(y == 0, core, 1 - core)
            row = lax.broadcasted_iota(jnp.int32, (BLK, 1), 0)
            pos_k = b * BLK + jnp.where(flip == 1, lax.rem(row + 64, BLK), row)
            seen = (pos_k <= qrow[x, 0:1, :]) & (pos_k >= qrow[x, 1:2, :])
            bias = jnp.where(seen, 0.0, NEG)
            body(t, x, y, g, jnp.concatenate([bias] * GROUP, axis=1))

        return 0

    lax.fori_loop(0, 6, step, 0)


def stat_tiles(info, qrow, qst, dst, chunk, s, state):
    k_ref, k_col, v_ref, v_col = chunk

    def body(t, x, y, g, bias):
        i = 2 * x + g
        rows = aligned(y, BLK)
        k = k_ref[pl.ds(rows, BLK), pl.ds(pl.multiple_of(k_col + g * DH, DH), DH)]
        v = v_ref[pl.ds(rows, BLK), pl.ds(pl.multiple_of(v_col + g * DH, DH), DH)]
        score = dot(k, qst[i], NT) * FACTOR + bias
        old = state[i, 0:1, :]
        new = jnp.maximum(old, jnp.max(score, axis=0, keepdims=True))
        p = jnp.exp2(score - new)
        grad = dot(v, dst[i], NT)
        alpha = jnp.exp2(old - new)
        state[i, 0:1, :] = new
        state[i, 1:2, :] = state[i, 1:2, :] * alpha + jnp.sum(p, axis=0, keepdims=True)
        state[i, 2:3, :] = state[i, 2:3, :] * alpha + jnp.sum(p * grad, axis=0, keepdims=True)

    for_tiles(info, qrow, s, body)


def grad_tiles(info, qrow, qst, dst, chunk, s, final, acc, dqt):
    k_ref, k_col, v_ref, v_col = chunk
    acc[...] = jnp.zeros_like(acc)

    def body(t, x, y, g, bias):
        i = 2 * x + g
        rows = aligned(y, BLK)
        k = k_ref[pl.ds(rows, BLK), pl.ds(pl.multiple_of(k_col + g * DH, DH), DH)]
        v = v_ref[pl.ds(rows, BLK), pl.ds(pl.multiple_of(v_col + g * DH, DH), DH)]
        w = jnp.exp2(dot(k, qst[i], NT) * FACTOR + bias - final[i, 0:1, :])
        ds = (w * (dot(v, dst[i], NT) - final[i, 1:2, :])).astype(BF16)
        acc[pl.ds(rows, BLK), pl.ds(aligned(g, DH), DH)] += dot(ds, qst[i], NN)
        acc[pl.ds(rows, BLK), pl.ds(pl.multiple_of(256 + g * DH, DH), DH)] += dot(
            w.astype(BF16), dst[i], NN
        )
        dqt[i] += dot(k, ds, TN)

    for_tiles(info, qrow, s, body)


def write_terms(acc, key_out, key_col, value_out, value_col):
    key_out[:, key_col:key_col + 256] = (acc[:, :256] * SCALE).astype(BF16)
    value_out[:, value_col:value_col + 256] = acc[:, 256:].astype(BF16)


def whole(ref):
    return (ref, 0, ref, 256)


def open_kernel(
    place, doc_ref, q_own, do_own, q_par, do_par, own, info, qrow, qst, dst, state, rows_in, sem
):
    info[0] = place[0]
    info[1] = place[1]
    low = aligned(place[0], 2048)
    copies = [
        pltpu.make_async_copy(source.at[:, pl.ds(low, 2048)], rows_in.at[i], sem.at[i])
        for i, source in enumerate((q_own, do_own, q_par, do_par))
    ]
    for one in copies:
        one.start()
    query_rows(doc_ref, info, qrow)
    for i, one in enumerate(copies):
        one.wait()
        out, part = (qst, dst)[i % 2], i // 2
        for x in range(2):
            for g in range(2):
                for h in range(GROUP):
                    cols = slice((g * GROUP + h) * DH, (g * GROUP + h + 1) * DH)
                    rows = slice(h * BLK + part * 64, h * BLK + part * 64 + 64)
                    out[2 * x + g, rows, :] = rows_in[i, x * 64:x * 64 + 64, cols]
    for i in range(4):
        state[i, 0:1, :] = jnp.full((1, LANES), LOW, F32)
        state[i, 1:3, :] = jnp.zeros((2, LANES), F32)
    stat_tiles(info, qrow, qst, dst, whole(own), info[1], state)


def stat_kernel(distance, info, qrow, qst, dst, up, down, state_in, state):
    state[...] = state_in[...]
    stat_tiles(info, qrow, qst, dst, whole(up), chip(info[1], -distance), state)
    stat_tiles(info, qrow, qst, dst, whole(down), chip(info[1], distance), state)


def far_kernel(
    info, qrow, qst, dst, far_k, far_v, state_in, final, tk, tv, ds_out,
    state, acc, probs, grads, maxes,
):
    state[...] = state_in[...]
    acc[...] = jnp.zeros_like(acc)
    s = chip(info[1], 4)

    def first(t, x, y, g, bias):
        i = 2 * x + g
        rows, cols = aligned(y, BLK), aligned(g, DH)
        score = dot(far_k[pl.ds(rows, BLK), pl.ds(cols, DH)], qst[i], NT) * FACTOR + bias
        old = state[i, 0:1, :]
        new = jnp.maximum(old, jnp.max(score, axis=0, keepdims=True))
        p = jnp.exp2(score - new)
        grad = dot(far_v[pl.ds(rows, BLK), pl.ds(cols, DH)], dst[i], NT)
        alpha = jnp.exp2(old - new)
        probs[t] = p
        grads[t] = grad
        maxes[t, 0:1, :] = new
        state[i, 0:1, :] = new
        state[i, 1:2, :] = state[i, 1:2, :] * alpha + jnp.sum(p, axis=0, keepdims=True)
        state[i, 2:3, :] = state[i, 2:3, :] * alpha + jnp.sum(p * grad, axis=0, keepdims=True)

    for_tiles(info, qrow, s, first)
    for i in range(4):
        total = state[i, 1:2, :]
        final[i, 0:1, :] = state[i, 0:1, :] + jnp.log2(total)
        final[i, 1:2, :] = state[i, 2:3, :] / total

    def second(t, x, y, g, bias):
        i = 2 * x + g
        rows, cols = aligned(y, BLK), aligned(g, DH)
        w = probs[t] * jnp.exp2(maxes[t, 0:1, :] - final[i, 0:1, :])
        ds = (w * (grads[t] - final[i, 1:2, :])).astype(BF16)
        ds_out[t] = ds
        acc[pl.ds(rows, BLK), pl.ds(cols, DH)] += dot(ds, qst[i], NN)
        acc[pl.ds(rows, BLK), pl.ds(pl.multiple_of(256 + g * DH, DH), DH)] += dot(
            w.astype(BF16), dst[i], NN
        )

    for_tiles(info, qrow, s, second)
    write_terms(acc, tk, 0, tv, 0)


def far_query(info, qrow, far_k, ds_in, dqt):
    def body(t, x, y, g, bias):
        k = far_k[pl.ds(aligned(y, BLK), BLK), pl.ds(aligned(g, DH), DH)]
        dqt[2 * x + g] += dot(k, ds_in[t], TN)

    for_tiles(info, qrow, chip(info[1], 4), body)


def third_kernel(info, qrow, qst, dst, up, down, final, tu, td, dqt, acc):
    dqt[...] = jnp.zeros_like(dqt)
    grad_pair(3, info, qrow, qst, dst, up, down, final, tu, td, dqt, acc)


def second_kernel(
    info, qrow, qst, dst, up, down, final, dqt_in, far_k, ds_in, tu, td, dqt, acc
):
    dqt[...] = dqt_in[...]
    grad_pair(2, info, qrow, qst, dst, up, down, final, tu, td, dqt, acc)
    far_query(info, qrow, far_k, ds_in, dqt)


def first_kernel(info, qrow, qst, dst, up, down, final, dqt_in, tu, td, dqt, acc):
    dqt[...] = dqt_in[...]
    grad_pair(1, info, qrow, qst, dst, up, down, final, tu, td, dqt, acc)


def grad_pair(distance, info, qrow, qst, dst, up, down, final, tu, td, dqt, acc):
    for chunk, out, offset in ((up, td, -distance), (down, tu, distance)):
        s = chip(info[1], offset)
        grad_tiles(info, qrow, qst, dst, whole(chunk), s, final, acc, dqt)
        write_terms(acc, out, 0, out, 256)


def close_kernel(info, qrow, qst, dst, own, final, dqt_in, t0, dq_own, dq_par, dqt, acc):
    dqt[...] = dqt_in[...]
    grad_tiles(info, qrow, qst, dst, whole(own), info[1], final, acc, dqt)
    write_terms(acc, t0, 0, t0, 256)
    for x in range(2):
        for g in range(2):
            for h in range(GROUP):
                part = dqt[2 * x + g, :, h * BLK:(h + 1) * BLK] * SCALE
                out = jnp.transpose(part).astype(BF16)
                cols = slice((g * GROUP + h) * DH, (g * GROUP + h + 1) * DH)
                dq_own[x * 64:x * 64 + 64, cols] = out[:64]
                dq_par[x * 64:x * 64 + 64, cols] = out[64:]


def assemble_kernel(place, mine, got, up, down, own):
    for part, source in ((0, mine), (64, got)):
        for out in (up, down, own):
            out[part:part + 64, :] = source[:64, :]
            out[BLK + part:BLK + part + 64, :] = source[64:, :]


def add_kernel(place, tu, td, up, down, up_out, down_out):
    width = up.shape[1]
    if width < 512:
        up_out[:, width:] = tu[:, width:]
        down_out[:, :512 - width] = td[:, :512 - width]
    cols = slice(0, width)
    up_out[:, cols] = (tu[:, cols].astype(F32) + up[...].astype(F32)).astype(BF16)
    cols = slice(512 - width, 512)
    down_out[:, cols] = (td[:, cols].astype(F32) + down[...].astype(F32)).astype(BF16)


def last_kernel(place, total, back, key, value, sem):
    core = place[0]
    mine, other = aligned(core, 256), aligned(1 - core, 256)
    copies = []
    for out, low in ((key, 0), (value, 256)):
        cols = pl.ds(low, 256)
        for source, target in (
            (total.at[pl.ds(0, 64), cols], out.at[pl.ds(0, 64), pl.ds(mine, 256)]),
            (total.at[pl.ds(128, 64), cols], out.at[pl.ds(64, 64), pl.ds(mine, 256)]),
            (back.at[:, cols], out.at[:, pl.ds(other, 256)]),
        ):
            copies.append(pltpu.make_async_copy(source, target, sem.at[len(copies)]))
            copies[-1].start()
    for one in copies:
        one.wait()


SMEM_SPEC = pl.BlockSpec(memory_space=pltpu.SMEM)
VMEM_SPEC = pl.BlockSpec(memory_space=pltpu.VMEM)
ANY_SPEC = pl.BlockSpec(memory_space=pltpu.HBM)


def shape(dims, dtype=BF16):
    return jax.ShapeDtypeStruct(dims, dtype)


INFO = shape((8,), jnp.int32)
QROW = shape((2, 8, BLK), jnp.int32)
STACK = shape((4, LANES, DH))
STATE = shape((4, 8, LANES), F32)
TERM = shape((256, 512))
HALF_TERM = shape((256, 256))
DQT = shape((4, DH, LANES), F32)
DQ = shape((BLK, 2048))


def call(kernel, out, args, scratch=(), cost=3, limit=24, first_out_smem=False, far=(), far_out=False):
    in_specs = [SMEM_SPEC] + [
        ANY_SPEC if i in far else VMEM_SPEC for i in range(1, len(args))
    ]
    specs = [ANY_SPEC if far_out else VMEM_SPEC] * len(out)
    if first_out_smem:
        specs[0] = SMEM_SPEC
    return pl.pallas_call(
        kernel,
        out_shape=tuple(out),
        in_specs=in_specs,
        out_specs=tuple(specs),
        scratch_shapes=list(scratch),
        compiler_params=pltpu.CompilerParams(vmem_limit_bytes=limit * MIB),
        cost_estimate=pl.CostEstimate(flops=cost * 10**9, bytes_accessed=10**6, transcendentals=0),
    )(*args)


SWAP = [(i, i ^ 1) for i in range(2 * NZ)]


def swap(x):
    return lax.ppermute(x, "ctx", SWAP)


def ring(x, step):
    pairs = [(2 * z + c, 2 * ((z + step) % NZ) + c) for z in range(NZ) for c in range(2)]
    return lax.ppermute(x, "ctx", pairs)


def half_of(x, index):
    width = x.shape[1] // 2
    return lax.dynamic_slice_in_dim(x, index * width, width, 1)


def join(mine, other, core):
    return jnp.where(
        core == 0,
        jnp.concatenate([mine, other], axis=1),
        jnp.concatenate([other, mine], axis=1),
    )


def add(a, b):
    return (a.astype(F32) + b.astype(F32)).astype(BF16)


def per_device(queries, key_states, value_states, grad_output, doc_ids):
    index = lax.axis_index("ctx")
    core, z = index % 2, index // 2
    place = jnp.stack([core, z]).astype(jnp.int32)
    doc = doc_ids.reshape(NB, BLK)

    mine = jnp.concatenate([half_of(key_states, core), half_of(value_states, core)], axis=1)
    other = jnp.concatenate([half_of(key_states, 1 - core), half_of(value_states, 1 - core)], axis=1)
    got = swap(other)
    own_up, own_down, own = call(assemble_kernel, [TERM] * 3, [place, mine, got])
    together = lax.optimization_barrier
    q_in, do_in, unused = together((queries, grad_output, got))
    q_par, do_par = swap(q_in), swap(do_in)
    up, down = ring(own_up, 1), ring(own_down, -1)
    info, qrow, qst, dst, state = call(
        open_kernel,
        [INFO, QROW, STACK, STACK, STATE],
        [place, doc, queries, grad_output, q_par, do_par, own],
        [pltpu.VMEM((4, BLK, 2048), BF16), pltpu.SemaphoreType.DMA((4,))],
        first_out_smem=True, far=(2, 3, 4, 5),
    )
    common = [info, qrow, qst, dst]
    ups, downs = [], []
    for k in (1, 2, 3):
        up, down, state = together((up, down, state))
        ups.append(up)
        downs.append(down)
        if k < 3:
            next_up, next_down = ring(up, 1), ring(down, -1)
        else:
            far_up, far_down = together((up[:, :256], down[:, 256:]))
            next_up, next_down = ring(far_up, 1), ring(far_down, -1)
        (state,) = call(
            functools.partial(stat_kernel, k), [STATE], common + [up, down, state]
        )
        up, down = next_up, next_down
    far_k, far_v = up, down
    acc = pltpu.VMEM((256, 512), F32)
    tiles = (6, BLK, LANES)
    final, tk, tv, ds_far = call(
        far_kernel, [STATE, HALF_TERM, HALF_TERM, shape(tiles)], common + [far_k, far_v, state],
        [pltpu.VMEM(STATE.shape, F32), acc, pltpu.VMEM(tiles, F32), pltpu.VMEM(tiles, F32),
         pltpu.VMEM((6, 8, LANES), F32)],
    )
    up, down = ring(tk, 1), ring(tv, -1)
    for k in (3, 2, 1):
        chunks = common + [ups[k - 1], downs[k - 1], final]
        outs = [TERM, TERM, DQT]
        if k == 3:
            tu, td, dqt = call(third_kernel, outs, chunks, [acc], cost=5)
        elif k == 2:
            tu, td, dqt = call(second_kernel, outs, chunks + [dqt, far_k, ds_far], [acc], cost=5)
        else:
            tu, td, dqt = call(first_kernel, outs, chunks + [dqt], [acc], cost=5)
        up, down, tu, td, dqt = together((up, down, tu, td, dqt))
        if k == 3:
            up = jnp.concatenate([add(tu[:, :256], up), tu[:, 256:]], axis=1)
            down = jnp.concatenate([td[:, :256], add(td[:, 256:], down)], axis=1)
        else:
            up, down = add(tu, up), add(td, down)
        up, down = together((up, down))
        up, down = ring(up, 1), ring(down, -1)
    t0, dq_own, dq_par = call(
        close_kernel, [TERM, DQ, DQ], common + [own, final, dqt],
        [pltpu.VMEM(DQT.shape, F32), acc], cost=5,
    )
    dq_got = swap(dq_par)
    total = (t0.astype(F32) + up.astype(F32) + down.astype(F32)).astype(BF16)
    away = jnp.concatenate([total[64:128], total[192:]], axis=0)
    away, dq_own = together((away, dq_own))
    back = swap(away)
    query_grad, total = together((join(dq_own, dq_got, core), total))
    key_grad, value_grad = call(
        last_kernel, [shape((BLK, 512))] * 2, [place, total, back],
        [pltpu.SemaphoreType.DMA((6,))], far_out=True,
    )
    return (query_grad, key_grad, value_grad)


def solution(mesh):
    rows = P(("dp", "ctx"), None)
    return jax.shard_map(
        per_device,
        mesh=mesh,
        in_specs=(rows, rows, rows, rows, P("dp")),
        out_specs=(rows, rows, rows),
        check_vma=False,
    )
```

```python
import functools

import jax
import jax.numpy as jnp
from jax import lax
from jax.experimental import pallas as pl
from jax.experimental.pallas import tpu as pltpu
from jax.sharding import PartitionSpec as P

DH = 128
GROUP = 8
SCALE = DH ** (-0.5)
FACTOR = SCALE * 1.4426950408889634
NEG = -1e30
LOW = -1e29
NZ = 8
BLK = 128
NB = 16
LANES = GROUP * BLK
MIB = 1024 * 1024
BF16 = jnp.bfloat16
F32 = jnp.float32

NT = (((1,), (1,)), ((), ()))
NN = (((1,), (0,)), ((), ()))
TN = (((0,), (0,)), ((), ()))


def dot(a, b, dims):
    return lax.dot_general(a, b, dims, preferred_element_type=F32)


def chip(z, offset):
    return lax.rem(z + offset + NZ, NZ)


def aligned(index, size):
    return pl.multiple_of(index * size, size)


def query_rows(doc_ref, info, qrow):
    core, z = info[0], info[1]
    doc = doc_ref[...]
    starts = [jnp.sum((doc < d).astype(F32)).astype(jnp.int32) for d in (1, 2, 3)]
    lane = lax.broadcasted_iota(jnp.int32, (1, BLK), 1)
    for x in range(2):
        block = z if x == 0 else NB - 1 - z
        flip = core if x == 0 else 1 - core
        rot = jnp.where(flip == 1, lax.rem(lane + 64, BLK), lane)
        doc_row = doc_ref[pl.ds(block, 1), :]
        doc_row = jnp.where(flip == 1, pltpu.roll(doc_row, 64, 1), doc_row)
        start = jnp.where(
            doc_row == 0, 0,
            jnp.where(doc_row == 1, starts[0], jnp.where(doc_row == 2, starts[1], starts[2])),
        )
        qrow[x, 0:1, :] = block * BLK + rot
        qrow[x, 1:2, :] = start
        info[2 + x] = lax.div(jnp.min(start), BLK)


def for_tiles(info, qrow, s, body):
    core, z = info[0], info[1]

    def step(t, unused):
        combo, g = lax.div(t, 2), lax.rem(t, 2)
        x, y = jnp.minimum(combo, 1), lax.div(combo, 2)
        b = jnp.where(y == 0, s, NB - 1 - s)
        qb = jnp.where(x == 0, z, NB - 1 - z)

        @pl.when((b <= qb) & (b >= info[2 + x]))
        def _():
            flip = jnp.where(y == 0, core, 1 - core)
            row = lax.broadcasted_iota(jnp.int32, (BLK, 1), 0)
            pos_k = b * BLK + jnp.where(flip == 1, lax.rem(row + 64, BLK), row)
            seen = (pos_k <= qrow[x, 0:1, :]) & (pos_k >= qrow[x, 1:2, :])
            bias = jnp.where(seen, 0.0, NEG)
            body(t, x, y, g, jnp.concatenate([bias] * GROUP, axis=1))

        return 0

    lax.fori_loop(0, 6, step, 0)


def stat_tiles(info, qrow, qst, dst, chunk, s, state):
    k_ref, k_col, v_ref, v_col = chunk

    def body(t, x, y, g, bias):
        i = 2 * x + g
        rows = aligned(y, BLK)
        k = k_ref[pl.ds(rows, BLK), pl.ds(pl.multiple_of(k_col + g * DH, DH), DH)]
        v = v_ref[pl.ds(rows, BLK), pl.ds(pl.multiple_of(v_col + g * DH, DH), DH)]
        score = dot(k, qst[i], NT) * FACTOR + bias
        old = state[i, 0:1, :]
        new = jnp.maximum(old, jnp.max(score, axis=0, keepdims=True))
        p = jnp.exp2(score - new)
        grad = dot(v, dst[i], NT)
        alpha = jnp.exp2(old - new)
        state[i, 0:1, :] = new
        state[i, 1:2, :] = state[i, 1:2, :] * alpha + jnp.sum(p, axis=0, keepdims=True)
        state[i, 2:3, :] = state[i, 2:3, :] * alpha + jnp.sum(p * grad, axis=0, keepdims=True)

    for_tiles(info, qrow, s, body)


def grad_tiles(info, qrow, qst, dst, chunk, s, final, acc, dqt):
    k_ref, k_col, v_ref, v_col = chunk
    acc[...] = jnp.zeros_like(acc)

    def body(t, x, y, g, bias):
        i = 2 * x + g
        rows = aligned(y, BLK)
        k = k_ref[pl.ds(rows, BLK), pl.ds(pl.multiple_of(k_col + g * DH, DH), DH)]
        v = v_ref[pl.ds(rows, BLK), pl.ds(pl.multiple_of(v_col + g * DH, DH), DH)]
        w = jnp.exp2(dot(k, qst[i], NT) * FACTOR + bias - final[i, 0:1, :])
        ds = (w * (dot(v, dst[i], NT) - final[i, 1:2, :])).astype(BF16)
        acc[pl.ds(rows, BLK), pl.ds(aligned(g, DH), DH)] += dot(ds, qst[i], NN)
        acc[pl.ds(rows, BLK), pl.ds(pl.multiple_of(256 + g * DH, DH), DH)] += dot(
            w.astype(BF16), dst[i], NN
        )
        dqt[i] += dot(k, ds, TN)

    for_tiles(info, qrow, s, body)


def write_terms(acc, key_out, key_col, value_out, value_col):
    key_out[:, key_col:key_col + 256] = (acc[:, :256] * SCALE).astype(BF16)
    value_out[:, value_col:value_col + 256] = acc[:, 256:].astype(BF16)


def whole(ref):
    return (ref, 0, ref, 256)


def open_kernel(
    place, doc_ref, q_own, do_own, q_par, do_par, own, info, qrow, qst, dst, state, rows_in, sem
):
    info[0] = place[0]
    info[1] = place[1]
    low = aligned(place[0], 2048)
    copies = [
        pltpu.make_async_copy(source.at[:, pl.ds(low, 2048)], rows_in.at[i], sem.at[i])
        for i, source in enumerate((q_own, do_own, q_par, do_par))
    ]
    for one in copies:
        one.start()
    query_rows(doc_ref, info, qrow)
    for i, one in enumerate(copies):
        one.wait()
        out, part = (qst, dst)[i % 2], i // 2
        for x in range(2):
            for g in range(2):
                for h in range(GROUP):
                    cols = slice((g * GROUP + h) * DH, (g * GROUP + h + 1) * DH)
                    rows = slice(h * BLK + part * 64, h * BLK + part * 64 + 64)
                    out[2 * x + g, rows, :] = rows_in[i, x * 64:x * 64 + 64, cols]
    for i in range(4):
        state[i, 0:1, :] = jnp.full((1, LANES), LOW, F32)
        state[i, 1:3, :] = jnp.zeros((2, LANES), F32)
    stat_tiles(info, qrow, qst, dst, whole(own), info[1], state)


def stat_kernel(distance, info, qrow, qst, dst, up, down, state_in, state):
    state[...] = state_in[...]
    stat_tiles(info, qrow, qst, dst, whole(up), chip(info[1], -distance), state)
    stat_tiles(info, qrow, qst, dst, whole(down), chip(info[1], distance), state)


def far_kernel(
    info, qrow, qst, dst, far_k, far_v, state_in, final, tk, tv, ds_out,
    state, acc, probs, grads, maxes,
):
    state[...] = state_in[...]
    acc[...] = jnp.zeros_like(acc)
    s = chip(info[1], 4)

    def first(t, x, y, g, bias):
        i = 2 * x + g
        rows, cols = aligned(y, BLK), aligned(g, DH)
        score = dot(far_k[pl.ds(rows, BLK), pl.ds(cols, DH)], qst[i], NT) * FACTOR + bias
        old = state[i, 0:1, :]
        new = jnp.maximum(old, jnp.max(score, axis=0, keepdims=True))
        p = jnp.exp2(score - new)
        grad = dot(far_v[pl.ds(rows, BLK), pl.ds(cols, DH)], dst[i], NT)
        alpha = jnp.exp2(old - new)
        probs[t] = p
        grads[t] = grad
        maxes[t, 0:1, :] = new
        state[i, 0:1, :] = new
        state[i, 1:2, :] = state[i, 1:2, :] * alpha + jnp.sum(p, axis=0, keepdims=True)
        state[i, 2:3, :] = state[i, 2:3, :] * alpha + jnp.sum(p * grad, axis=0, keepdims=True)

    for_tiles(info, qrow, s, first)
    for i in range(4):
        total = state[i, 1:2, :]
        final[i, 0:1, :] = state[i, 0:1, :] + jnp.log2(total)
        final[i, 1:2, :] = state[i, 2:3, :] / total

    def second(t, x, y, g, bias):
        i = 2 * x + g
        rows, cols = aligned(y, BLK), aligned(g, DH)
        w = probs[t] * jnp.exp2(maxes[t, 0:1, :] - final[i, 0:1, :])
        ds = (w * (grads[t] - final[i, 1:2, :])).astype(BF16)
        ds_out[t] = ds
        acc[pl.ds(rows, BLK), pl.ds(cols, DH)] += dot(ds, qst[i], NN)
        acc[pl.ds(rows, BLK), pl.ds(pl.multiple_of(256 + g * DH, DH), DH)] += dot(
            w.astype(BF16), dst[i], NN
        )

    for_tiles(info, qrow, s, second)
    write_terms(acc, tk, 0, tv, 0)


def far_query(info, qrow, far_k, ds_in, dqt):
    def body(t, x, y, g, bias):
        k = far_k[pl.ds(aligned(y, BLK), BLK), pl.ds(aligned(g, DH), DH)]
        dqt[2 * x + g] += dot(k, ds_in[t], TN)

    for_tiles(info, qrow, chip(info[1], 4), body)


def third_kernel(info, qrow, qst, dst, up, down, final, tu, td, dqt, acc):
    dqt[...] = jnp.zeros_like(dqt)
    grad_pair(3, info, qrow, qst, dst, up, down, final, tu, td, dqt, acc)


def second_kernel(
    info, qrow, qst, dst, up, down, final, dqt_in, far_k, ds_in, tu, td, dqt, acc
):
    dqt[...] = dqt_in[...]
    grad_pair(2, info, qrow, qst, dst, up, down, final, tu, td, dqt, acc)
    far_query(info, qrow, far_k, ds_in, dqt)


def first_kernel(info, qrow, qst, dst, up, down, final, dqt_in, tu, td, dqt, acc):
    dqt[...] = dqt_in[...]
    grad_pair(1, info, qrow, qst, dst, up, down, final, tu, td, dqt, acc)


def grad_pair(distance, info, qrow, qst, dst, up, down, final, tu, td, dqt, acc):
    for chunk, out, offset in ((up, td, -distance), (down, tu, distance)):
        s = chip(info[1], offset)
        grad_tiles(info, qrow, qst, dst, whole(chunk), s, final, acc, dqt)
        write_terms(acc, out, 0, out, 256)


def close_kernel(info, qrow, qst, dst, own, final, dqt_in, t0, dq_own, dq_par, dqt, acc):
    dqt[...] = dqt_in[...]
    grad_tiles(info, qrow, qst, dst, whole(own), info[1], final, acc, dqt)
    write_terms(acc, t0, 0, t0, 256)
    for x in range(2):
        for g in range(2):
            for h in range(GROUP):
                part = dqt[2 * x + g, :, h * BLK:(h + 1) * BLK] * SCALE
                out = jnp.transpose(part).astype(BF16)
                cols = slice((g * GROUP + h) * DH, (g * GROUP + h + 1) * DH)
                dq_own[x * 64:x * 64 + 64, cols] = out[:64]
                dq_par[x * 64:x * 64 + 64, cols] = out[64:]


def assemble_kernel(place, mine, got, up, down, own):
    for part, source in ((0, mine), (64, got)):
        for out in (up, down, own):
            out[part:part + 64, :] = source[:64, :]
            out[BLK + part:BLK + part + 64, :] = source[64:, :]


def add_kernel(place, tu, td, up, down, up_out, down_out):
    width = up.shape[1]
    if width < 512:
        up_out[:, width:] = tu[:, width:]
        down_out[:, :512 - width] = td[:, :512 - width]
    cols = slice(0, width)
    up_out[:, cols] = (tu[:, cols].astype(F32) + up[...].astype(F32)).astype(BF16)
    cols = slice(512 - width, 512)
    down_out[:, cols] = (td[:, cols].astype(F32) + down[...].astype(F32)).astype(BF16)


def last_kernel(place, t0, up, down, back, key, value, total, sem):
    core = place[0]
    for row in (0, 128):
        rows = slice(row, row + 64)
        part = t0[rows, :].astype(F32) + up[rows, :].astype(F32) + down[rows, :].astype(F32)
        total[rows, :] = part.astype(BF16)
    mine, other = aligned(core, 256), aligned(1 - core, 256)
    copies = []
    for out, low in ((key, 0), (value, 256)):
        cols = pl.ds(low, 256)
        for source, target in (
            (total.at[pl.ds(0, 64), cols], out.at[pl.ds(0, 64), pl.ds(mine, 256)]),
            (total.at[pl.ds(128, 64), cols], out.at[pl.ds(64, 64), pl.ds(mine, 256)]),
            (back.at[:, cols], out.at[:, pl.ds(other, 256)]),
        ):
            copies.append(pltpu.make_async_copy(source, target, sem.at[len(copies)]))
            copies[-1].start()
    for one in copies:
        one.wait()


SMEM_SPEC = pl.BlockSpec(memory_space=pltpu.SMEM)
VMEM_SPEC = pl.BlockSpec(memory_space=pltpu.VMEM)
ANY_SPEC = pl.BlockSpec(memory_space=pltpu.HBM)


def shape(dims, dtype=BF16):
    return jax.ShapeDtypeStruct(dims, dtype)


INFO = shape((8,), jnp.int32)
QROW = shape((2, 8, BLK), jnp.int32)
STACK = shape((4, LANES, DH))
STATE = shape((4, 8, LANES), F32)
TERM = shape((256, 512))
HALF_TERM = shape((256, 256))
DQT = shape((4, DH, LANES), F32)
DQ = shape((BLK, 2048))


def call(kernel, out, args, scratch=(), cost=3, limit=24, first_out_smem=False, far=(), far_out=False):
    in_specs = [SMEM_SPEC] + [
        ANY_SPEC if i in far else VMEM_SPEC for i in range(1, len(args))
    ]
    specs = [ANY_SPEC if far_out else VMEM_SPEC] * len(out)
    if first_out_smem:
        specs[0] = SMEM_SPEC
    return pl.pallas_call(
        kernel,
        out_shape=tuple(out),
        in_specs=in_specs,
        out_specs=tuple(specs),
        scratch_shapes=list(scratch),
        compiler_params=pltpu.CompilerParams(vmem_limit_bytes=limit * MIB),
        cost_estimate=pl.CostEstimate(flops=cost * 10**9, bytes_accessed=10**6, transcendentals=0),
    )(*args)


SWAP = [(i, i ^ 1) for i in range(2 * NZ)]


def swap(x):
    return lax.ppermute(x, "ctx", SWAP)


def ring(x, step):
    pairs = [(2 * z + c, 2 * ((z + step) % NZ) + c) for z in range(NZ) for c in range(2)]
    return lax.ppermute(x, "ctx", pairs)


def half_of(x, index):
    width = x.shape[1] // 2
    return lax.dynamic_slice_in_dim(x, index * width, width, 1)


def join(mine, other, core):
    return jnp.where(
        core == 0,
        jnp.concatenate([mine, other], axis=1),
        jnp.concatenate([other, mine], axis=1),
    )


def add(a, b):
    return (a.astype(F32) + b.astype(F32)).astype(BF16)


def per_device(queries, key_states, value_states, grad_output, doc_ids):
    index = lax.axis_index("ctx")
    core, z = index % 2, index // 2
    place = jnp.stack([core, z]).astype(jnp.int32)
    doc = doc_ids.reshape(NB, BLK)

    mine = jnp.concatenate([half_of(key_states, core), half_of(value_states, core)], axis=1)
    other = jnp.concatenate([half_of(key_states, 1 - core), half_of(value_states, 1 - core)], axis=1)
    got = swap(other)
    own_up, own_down, own = call(assemble_kernel, [TERM] * 3, [place, mine, got])
    together = lax.optimization_barrier
    q_in, do_in, unused = together((queries, grad_output, got))
    q_par, do_par = swap(q_in), swap(do_in)
    up, down = ring(own_up, 1), ring(own_down, -1)
    info, qrow, qst, dst, state = call(
        open_kernel,
        [INFO, QROW, STACK, STACK, STATE],
        [place, doc, queries, grad_output, q_par, do_par, own],
        [pltpu.VMEM((4, BLK, 2048), BF16), pltpu.SemaphoreType.DMA((4,))],
        first_out_smem=True, far=(2, 3, 4, 5),
    )
    common = [info, qrow, qst, dst]
    ups, downs = [], []
    for k in (1, 2, 3):
        up, down, state = together((up, down, state))
        ups.append(up)
        downs.append(down)
        if k < 3:
            next_up, next_down = ring(up, 1), ring(down, -1)
        else:
            far_up, far_down = together((up[:, :256], down[:, 256:]))
            next_up, next_down = ring(far_up, 1), ring(far_down, -1)
        (state,) = call(
            functools.partial(stat_kernel, k), [STATE], common + [up, down, state]
        )
        up, down = next_up, next_down
    far_k, far_v = up, down
    acc = pltpu.VMEM((256, 512), F32)
    tiles = (6, BLK, LANES)
    final, tk, tv, ds_far = call(
        far_kernel, [STATE, HALF_TERM, HALF_TERM, shape(tiles)], common + [far_k, far_v, state],
        [pltpu.VMEM(STATE.shape, F32), acc, pltpu.VMEM(tiles, F32), pltpu.VMEM(tiles, F32),
         pltpu.VMEM((6, 8, LANES), F32)],
    )
    up, down = ring(tk, 1), ring(tv, -1)
    for k in (3, 2, 1):
        chunks = common + [ups[k - 1], downs[k - 1], final]
        outs = [TERM, TERM, DQT]
        if k == 3:
            tu, td, dqt = call(third_kernel, outs, chunks, [acc], cost=5)
        elif k == 2:
            tu, td, dqt = call(second_kernel, outs, chunks + [dqt, far_k, ds_far], [acc], cost=5)
        else:
            tu, td, dqt = call(first_kernel, outs, chunks + [dqt], [acc], cost=5)
        up, down, tu, td, dqt = together((up, down, tu, td, dqt))
        if k == 3:
            up = jnp.concatenate([add(tu[:, :256], up), tu[:, 256:]], axis=1)
            down = jnp.concatenate([td[:, :256], add(td[:, 256:], down)], axis=1)
        else:
            up, down = add(tu, up), add(td, down)
        up, down = together((up, down))
        up, down = ring(up, 1), ring(down, -1)
    t0, dq_own, dq_par = call(
        close_kernel, [TERM, DQ, DQ], common + [own, final, dqt],
        [pltpu.VMEM(DQT.shape, F32), acc], cost=5,
    )
    dq_got = swap(dq_par)
    away = jnp.concatenate(
        [sum(x[row:row + 64].astype(F32) for x in (t0, up, down)).astype(BF16) for row in (64, 192)],
        axis=0,
    )
    away, dq_own = together((away, dq_own))
    back = swap(away)
    query_grad, up = together((join(dq_own, dq_got, core), up))
    key_grad, value_grad = call(
        last_kernel, [shape((BLK, 512))] * 2, [place, t0, up, down, back],
        [pltpu.VMEM(TERM.shape, BF16), pltpu.SemaphoreType.DMA((6,))], far_out=True,
    )
    return (query_grad, key_grad, value_grad)


def solution(mesh):
    rows = P(("dp", "ctx"), None)
    return jax.shard_map(
        per_device,
        mesh=mesh,
        in_specs=(rows, rows, rows, rows, P("dp")),
        out_specs=(rows, rows, rows),
        check_vma=False,
    )
```

```python
import functools

import jax
import jax.numpy as jnp
from jax import lax
from jax.experimental import pallas as pl
from jax.experimental.pallas import tpu as pltpu
from jax.sharding import PartitionSpec as P

DH = 128
GROUP = 8
SCALE = DH ** (-0.5)
FACTOR = SCALE * 1.4426950408889634
NEG = -1e30
LOW = -1e29
NZ = 8
BLK = 128
NB = 16
LANES = GROUP * BLK
MIB = 1024 * 1024
BF16 = jnp.bfloat16
F32 = jnp.float32

NT = (((1,), (1,)), ((), ()))
NN = (((1,), (0,)), ((), ()))
TN = (((0,), (0,)), ((), ()))


def dot(a, b, dims):
    return lax.dot_general(a, b, dims, preferred_element_type=F32)


def chip(z, offset):
    return lax.rem(z + offset + NZ, NZ)


def aligned(index, size):
    return pl.multiple_of(index * size, size)


def query_rows(doc_ref, info, qrow):
    core, z = info[0], info[1]
    doc = doc_ref[...]
    starts = [jnp.sum((doc < d).astype(F32)).astype(jnp.int32) for d in (1, 2, 3)]
    lane = lax.broadcasted_iota(jnp.int32, (1, BLK), 1)
    for x in range(2):
        block = z if x == 0 else NB - 1 - z
        flip = core if x == 0 else 1 - core
        rot = jnp.where(flip == 1, lax.rem(lane + 64, BLK), lane)
        doc_row = doc_ref[pl.ds(block, 1), :]
        doc_row = jnp.where(flip == 1, pltpu.roll(doc_row, 64, 1), doc_row)
        start = jnp.where(
            doc_row == 0, 0,
            jnp.where(doc_row == 1, starts[0], jnp.where(doc_row == 2, starts[1], starts[2])),
        )
        qrow[x, 0:1, :] = block * BLK + rot
        qrow[x, 1:2, :] = start
        info[2 + x] = lax.div(jnp.min(start), BLK)


def for_tiles(info, qrow, s, body):
    core, z = info[0], info[1]

    def step(t, unused):
        combo, g = lax.div(t, 2), lax.rem(t, 2)
        x, y = jnp.minimum(combo, 1), lax.div(combo, 2)
        b = jnp.where(y == 0, s, NB - 1 - s)
        qb = jnp.where(x == 0, z, NB - 1 - z)

        @pl.when((b <= qb) & (b >= info[2 + x]))
        def _():
            flip = jnp.where(y == 0, core, 1 - core)
            row = lax.broadcasted_iota(jnp.int32, (BLK, 1), 0)
            pos_k = b * BLK + jnp.where(flip == 1, lax.rem(row + 64, BLK), row)
            seen = (pos_k <= qrow[x, 0:1, :]) & (pos_k >= qrow[x, 1:2, :])
            bias = jnp.where(seen, 0.0, NEG)
            body(t, x, y, g, jnp.concatenate([bias] * GROUP, axis=1))

        return 0

    lax.fori_loop(0, 6, step, 0)


def stat_tiles(info, qrow, qst, dst, chunk, s, state):
    k_ref, k_col, v_ref, v_col = chunk

    def body(t, x, y, g, bias):
        i = 2 * x + g
        rows = aligned(y, BLK)
        k = k_ref[pl.ds(rows, BLK), pl.ds(pl.multiple_of(k_col + g * DH, DH), DH)]
        v = v_ref[pl.ds(rows, BLK), pl.ds(pl.multiple_of(v_col + g * DH, DH), DH)]
        score = dot(k, qst[i], NT) * FACTOR + bias
        old = state[i, 0:1, :]
        new = jnp.maximum(old, jnp.max(score, axis=0, keepdims=True))
        p = jnp.exp2(score - new)
        grad = dot(v, dst[i], NT)
        alpha = jnp.exp2(old - new)
        state[i, 0:1, :] = new
        state[i, 1:2, :] = state[i, 1:2, :] * alpha + jnp.sum(p, axis=0, keepdims=True)
        state[i, 2:3, :] = state[i, 2:3, :] * alpha + jnp.sum(p * grad, axis=0, keepdims=True)

    for_tiles(info, qrow, s, body)


def grad_tiles(info, qrow, qst, dst, chunk, s, final, acc, dqt):
    k_ref, k_col, v_ref, v_col = chunk
    acc[...] = jnp.zeros_like(acc)

    def body(t, x, y, g, bias):
        i = 2 * x + g
        rows = aligned(y, BLK)
        k = k_ref[pl.ds(rows, BLK), pl.ds(pl.multiple_of(k_col + g * DH, DH), DH)]
        v = v_ref[pl.ds(rows, BLK), pl.ds(pl.multiple_of(v_col + g * DH, DH), DH)]
        w = jnp.exp2(dot(k, qst[i], NT) * FACTOR + bias - final[i, 0:1, :])
        ds = (w * (dot(v, dst[i], NT) - final[i, 1:2, :])).astype(BF16)
        acc[pl.ds(rows, BLK), pl.ds(aligned(g, DH), DH)] += dot(ds, qst[i], NN)
        acc[pl.ds(rows, BLK), pl.ds(pl.multiple_of(256 + g * DH, DH), DH)] += dot(
            w.astype(BF16), dst[i], NN
        )
        dqt[i] += dot(k, ds, TN)

    for_tiles(info, qrow, s, body)


def write_terms(acc, key_out, key_col, value_out, value_col):
    key_out[:, key_col:key_col + 256] = (acc[:, :256] * SCALE).astype(BF16)
    value_out[:, value_col:value_col + 256] = acc[:, 256:].astype(BF16)


def whole(ref):
    return (ref, 0, ref, 256)


def open_kernel(
    place, doc_ref, q_own, do_own, q_par, do_par, own, info, qrow, qst, dst, state, rows_in, sem
):
    info[0] = place[0]
    info[1] = place[1]
    low = aligned(place[0], 2048)
    copies = [
        pltpu.make_async_copy(source.at[:, pl.ds(low, 2048)], rows_in.at[i], sem.at[i])
        for i, source in enumerate((q_own, do_own, q_par, do_par))
    ]
    for one in copies:
        one.start()
    query_rows(doc_ref, info, qrow)
    for i, one in enumerate(copies):
        one.wait()
        out, part = (qst, dst)[i % 2], i // 2
        for x in range(2):
            for g in range(2):
                for h in range(GROUP):
                    cols = slice((g * GROUP + h) * DH, (g * GROUP + h + 1) * DH)
                    rows = slice(h * BLK + part * 64, h * BLK + part * 64 + 64)
                    out[2 * x + g, rows, :] = rows_in[i, x * 64:x * 64 + 64, cols]
    for i in range(4):
        state[i, 0:1, :] = jnp.full((1, LANES), LOW, F32)
        state[i, 1:3, :] = jnp.zeros((2, LANES), F32)
    stat_tiles(info, qrow, qst, dst, whole(own), info[1], state)


def stat_kernel(distance, info, qrow, qst, dst, up, down, state_in, state):
    state[...] = state_in[...]
    stat_tiles(info, qrow, qst, dst, whole(up), chip(info[1], -distance), state)
    stat_tiles(info, qrow, qst, dst, whole(down), chip(info[1], distance), state)


def far_kernel(
    info, qrow, qst, dst, far_k, far_v, state_in, final, tk, tv, ds_out,
    state, acc, probs, grads, maxes,
):
    state[...] = state_in[...]
    acc[...] = jnp.zeros_like(acc)
    s = chip(info[1], 4)

    def first(t, x, y, g, bias):
        i = 2 * x + g
        rows, cols = aligned(y, BLK), aligned(g, DH)
        score = dot(far_k[pl.ds(rows, BLK), pl.ds(cols, DH)], qst[i], NT) * FACTOR + bias
        old = state[i, 0:1, :]
        new = jnp.maximum(old, jnp.max(score, axis=0, keepdims=True))
        p = jnp.exp2(score - new)
        grad = dot(far_v[pl.ds(rows, BLK), pl.ds(cols, DH)], dst[i], NT)
        alpha = jnp.exp2(old - new)
        probs[t] = p
        grads[t] = grad
        maxes[t, 0:1, :] = new
        state[i, 0:1, :] = new
        state[i, 1:2, :] = state[i, 1:2, :] * alpha + jnp.sum(p, axis=0, keepdims=True)
        state[i, 2:3, :] = state[i, 2:3, :] * alpha + jnp.sum(p * grad, axis=0, keepdims=True)

    for_tiles(info, qrow, s, first)
    for i in range(4):
        total = state[i, 1:2, :]
        final[i, 0:1, :] = state[i, 0:1, :] + jnp.log2(total)
        final[i, 1:2, :] = state[i, 2:3, :] / total

    def second(t, x, y, g, bias):
        i = 2 * x + g
        rows, cols = aligned(y, BLK), aligned(g, DH)
        w = probs[t] * jnp.exp2(maxes[t, 0:1, :] - final[i, 0:1, :])
        ds = (w * (grads[t] - final[i, 1:2, :])).astype(BF16)
        ds_out[t] = ds
        acc[pl.ds(rows, BLK), pl.ds(cols, DH)] += dot(ds, qst[i], NN)
        acc[pl.ds(rows, BLK), pl.ds(pl.multiple_of(256 + g * DH, DH), DH)] += dot(
            w.astype(BF16), dst[i], NN
        )

    for_tiles(info, qrow, s, second)
    write_terms(acc, tk, 0, tv, 0)


def far_query(info, qrow, far_k, ds_in, dqt):
    def body(t, x, y, g, bias):
        k = far_k[pl.ds(aligned(y, BLK), BLK), pl.ds(aligned(g, DH), DH)]
        dqt[2 * x + g] += dot(k, ds_in[t], TN)

    for_tiles(info, qrow, chip(info[1], 4), body)


def third_kernel(info, qrow, qst, dst, up, down, final, tu, td, dqt, acc):
    dqt[...] = jnp.zeros_like(dqt)
    grad_pair(3, info, qrow, qst, dst, up, down, final, tu, td, dqt, acc)


def second_kernel(
    info, qrow, qst, dst, up, down, final, dqt_in, far_k, ds_in, tu, td, dqt, acc
):
    dqt[...] = dqt_in[...]
    grad_pair(2, info, qrow, qst, dst, up, down, final, tu, td, dqt, acc)
    far_query(info, qrow, far_k, ds_in, dqt)


def first_kernel(info, qrow, qst, dst, up, down, final, dqt_in, tu, td, dqt, acc):
    dqt[...] = dqt_in[...]
    grad_pair(1, info, qrow, qst, dst, up, down, final, tu, td, dqt, acc)


def grad_pair(distance, info, qrow, qst, dst, up, down, final, tu, td, dqt, acc):
    for chunk, out, offset in ((up, td, -distance), (down, tu, distance)):
        s = chip(info[1], offset)
        grad_tiles(info, qrow, qst, dst, whole(chunk), s, final, acc, dqt)
        write_terms(acc, out, 0, out, 256)


def close_kernel(info, qrow, qst, dst, own, final, dqt_in, t0, dq_own, dq_par, dqt, acc):
    dqt[...] = dqt_in[...]
    grad_tiles(info, qrow, qst, dst, whole(own), info[1], final, acc, dqt)
    write_terms(acc, t0, 0, t0, 256)
    for x in range(2):
        for g in range(2):
            for h in range(GROUP):
                part = dqt[2 * x + g, :, h * BLK:(h + 1) * BLK] * SCALE
                out = jnp.transpose(part).astype(BF16)
                cols = slice((g * GROUP + h) * DH, (g * GROUP + h + 1) * DH)
                dq_own[x * 64:x * 64 + 64, cols] = out[:64]
                dq_par[x * 64:x * 64 + 64, cols] = out[64:]


def assemble_kernel(place, mine, got, up, down, own):
    for part, source in ((0, mine), (64, got)):
        for out in (up, down, own):
            out[part:part + 64, :] = source[:64, :]
            out[BLK + part:BLK + part + 64, :] = source[64:, :]


def add_kernel(place, tu, td, up, down, up_out, down_out):
    width = up.shape[1]
    if width < 512:
        up_out[:, width:] = tu[:, width:]
        down_out[:, :512 - width] = td[:, :512 - width]
    cols = slice(0, width)
    up_out[:, cols] = (tu[:, cols].astype(F32) + up[...].astype(F32)).astype(BF16)
    cols = slice(512 - width, 512)
    down_out[:, cols] = (td[:, cols].astype(F32) + down[...].astype(F32)).astype(BF16)


def last_kernel(place, total, back, key, value, sem):
    core = place[0]
    mine, other = aligned(core, 256), aligned(1 - core, 256)
    copies = []
    for out, low in ((key, 0), (value, 256)):
        cols = pl.ds(low, 256)
        for source, target in (
            (total.at[pl.ds(0, 64), cols], out.at[pl.ds(0, 64), pl.ds(mine, 256)]),
            (total.at[pl.ds(128, 64), cols], out.at[pl.ds(64, 64), pl.ds(mine, 256)]),
            (back.at[:, cols], out.at[:, pl.ds(other, 256)]),
        ):
            copies.append(pltpu.make_async_copy(source, target, sem.at[len(copies)]))
            copies[-1].start()
    for one in copies:
        one.wait()


SMEM_SPEC = pl.BlockSpec(memory_space=pltpu.SMEM)
VMEM_SPEC = pl.BlockSpec(memory_space=pltpu.VMEM)
ANY_SPEC = pl.BlockSpec(memory_space=pltpu.HBM)


def shape(dims, dtype=BF16):
    return jax.ShapeDtypeStruct(dims, dtype)


INFO = shape((8,), jnp.int32)
QROW = shape((2, 8, BLK), jnp.int32)
STACK = shape((4, LANES, DH))
STATE = shape((4, 8, LANES), F32)
TERM = shape((256, 512))
HALF_TERM = shape((256, 256))
DQT = shape((4, DH, LANES), F32)
DQ = shape((BLK, 2048))


def call(kernel, out, args, scratch=(), cost=3, limit=24, first_out_smem=False, far=(), far_out=False):
    in_specs = [SMEM_SPEC] + [
        ANY_SPEC if i in far else VMEM_SPEC for i in range(1, len(args))
    ]
    specs = [ANY_SPEC if far_out else VMEM_SPEC] * len(out)
    if first_out_smem:
        specs[0] = SMEM_SPEC
    return pl.pallas_call(
        kernel,
        out_shape=tuple(out),
        in_specs=in_specs,
        out_specs=tuple(specs),
        scratch_shapes=list(scratch),
        compiler_params=pltpu.CompilerParams(vmem_limit_bytes=limit * MIB),
        cost_estimate=pl.CostEstimate(flops=cost * 10**9, bytes_accessed=10**6, transcendentals=0),
    )(*args)


SWAP = [(i, i ^ 1) for i in range(2 * NZ)]


def swap(x):
    return lax.ppermute(x, "ctx", SWAP)


def cross_ring(x, step):
    pairs = [
        (2 * z + c, 2 * ((z + step * (1 - 2 * c)) % NZ) + c) for z in range(NZ) for c in range(2)
    ]
    return lax.ppermute(x, "ctx", pairs)


def ring(x, step):
    pairs = [(2 * z + c, 2 * ((z + step) % NZ) + c) for z in range(NZ) for c in range(2)]
    return lax.ppermute(x, "ctx", pairs)


def half_of(x, index):
    width = x.shape[1] // 2
    return lax.dynamic_slice_in_dim(x, index * width, width, 1)


def join(mine, other, core):
    return jnp.where(
        core == 0,
        jnp.concatenate([mine, other], axis=1),
        jnp.concatenate([other, mine], axis=1),
    )


def add(a, b):
    return (a.astype(F32) + b.astype(F32)).astype(BF16)


def per_device(queries, key_states, value_states, grad_output, doc_ids):
    index = lax.axis_index("ctx")
    core, z = index % 2, index // 2
    place = jnp.stack([core, z]).astype(jnp.int32)
    doc = doc_ids.reshape(NB, BLK)

    mine = jnp.concatenate([half_of(key_states, core), half_of(value_states, core)], axis=1)
    other = jnp.concatenate([half_of(key_states, 1 - core), half_of(value_states, 1 - core)], axis=1)
    got = swap(other)
    own_up, own_down, own = call(assemble_kernel, [TERM] * 3, [place, mine, got])
    together = lax.optimization_barrier
    q_in, do_in, unused = together((queries, grad_output, got))
    q_par, do_par = swap(q_in), swap(do_in)
    up, down = cross_ring(own_up, 1), cross_ring(own_down, -1)
    info, qrow, qst, dst, state = call(
        open_kernel,
        [INFO, QROW, STACK, STACK, STATE],
        [place, doc, queries, grad_output, q_par, do_par, own],
        [pltpu.VMEM((4, BLK, 2048), BF16), pltpu.SemaphoreType.DMA((4,))],
        first_out_smem=True, far=(2, 3, 4, 5),
    )
    common = [info, qrow, qst, dst]
    ups, downs = [], []
    for k in (1, 2, 3):
        up, down, state = together((up, down, state))
        if k == 1:
            up, down = together((jnp.where(core == 0, up, down), jnp.where(core == 0, down, up)))
        ups.append(up)
        downs.append(down)
        if k < 3:
            next_up, next_down = ring(up, 1), ring(down, -1)
        else:
            far_up, far_down = together((up[:, :256], down[:, 256:]))
            next_up, next_down = ring(far_up, 1), ring(far_down, -1)
        (state,) = call(
            functools.partial(stat_kernel, k), [STATE], common + [up, down, state]
        )
        up, down = next_up, next_down
    far_k, far_v = up, down
    acc = pltpu.VMEM((256, 512), F32)
    tiles = (6, BLK, LANES)
    final, tk, tv, ds_far = call(
        far_kernel, [STATE, HALF_TERM, HALF_TERM, shape(tiles)], common + [far_k, far_v, state],
        [pltpu.VMEM(STATE.shape, F32), acc, pltpu.VMEM(tiles, F32), pltpu.VMEM(tiles, F32),
         pltpu.VMEM((6, 8, LANES), F32)],
    )
    up, down = ring(tk, 1), ring(tv, -1)
    for k in (3, 2, 1):
        chunks = common + [ups[k - 1], downs[k - 1], final]
        outs = [TERM, TERM, DQT]
        if k == 3:
            tu, td, dqt = call(third_kernel, outs, chunks, [acc], cost=5)
        elif k == 2:
            tu, td, dqt = call(second_kernel, outs, chunks + [dqt, far_k, ds_far], [acc], cost=5)
        else:
            tu, td, dqt = call(first_kernel, outs, chunks + [dqt], [acc], cost=5)
        up, down, tu, td, dqt = together((up, down, tu, td, dqt))
        if k == 3:
            up = jnp.concatenate([add(tu[:, :256], up), tu[:, 256:]], axis=1)
            down = jnp.concatenate([td[:, :256], add(td[:, 256:], down)], axis=1)
        else:
            up, down = add(tu, up), add(td, down)
        up, down = together((up, down))
        up, down = ring(up, 1), ring(down, -1)
    t0, dq_own, dq_par = call(
        close_kernel, [TERM, DQ, DQ], common + [own, final, dqt],
        [pltpu.VMEM(DQT.shape, F32), acc], cost=5,
    )
    dq_got = swap(dq_par)
    total = (t0.astype(F32) + up.astype(F32) + down.astype(F32)).astype(BF16)
    away = jnp.concatenate([total[64:128], total[192:]], axis=0)
    away, dq_own = together((away, dq_own))
    back = swap(away)
    query_grad, total = together((join(dq_own, dq_got, core), total))
    key_grad, value_grad = call(
        last_kernel, [shape((BLK, 512))] * 2, [place, total, back],
        [pltpu.SemaphoreType.DMA((6,))], far_out=True,
    )
    return (query_grad, key_grad, value_grad)


def solution(mesh):
    rows = P(("dp", "ctx"), None)
    return jax.shard_map(
        per_device,
        mesh=mesh,
        in_specs=(rows, rows, rows, rows, P("dp")),
        out_specs=(rows, rows, rows),
        check_vma=False,
    )
```
